32 devices in a mesh: row: 4 (over y, x), col: 8 (over z, core).
Axes of the slice: x: 2, y: 2, z: 4, core: 2. Of those that a mesh axis runs over, the one named last changes fastest.
Arguments:
- features: bfloat16 [8192, 256], P(('row', 'col')), may hold values from -6 to 6
- weight: bfloat16 [256, 256], replicated, may hold values from -0.375 to 0.375
- cotangent: bfloat16 [8192, 256], P(('row', 'col')), may hold values from -6 to 6
- tiles: int32 [4, 8, 2, 64], P('row', 'col'), may hold values from 0 to 15, as said below
- tile_count: int32 [4, 8], P('row', 'col'), may hold values from 8 to 64, as said below
- patterns: int32 [4, 8, 64, 16, 128], P('row', 'col'), may hold values from 0 to 255
Outputs:
- activated: bfloat16 [8192, 256], P(('row', 'col'))
- grad_features: bfloat16 [8192, 256], P(('row', 'col'))
- grad_weight: float32 [256, 256], replicated
The draws below stay inside these ranges and needn't reach their ends.
Inputs may be any that keep to these rules, and one draw needn't show every extreme that they name: `tiles`: on each device the slots name distinct pairs (block row a among its 16 block rows, block column b among its 8 block columns); slots at or after tile_count are not part of S. `tile_count`: live slots of one device; some device has exactly 64 in every draw.
All inputs are finite; a program needn't handle non-finite values.
Results may differ from the reference program's by a relative error of at most 0.018.
Values may be sent and summed in bfloat16 or wider, within the bound.
No kernel may reach another device: no remote copies, remote signals or barrier semaphores. Data moves between devices by JAX's collectives and lax.ppermute only.
A program may use at most 64 MiB of HBM per device.

```python
import jax
import jax.numpy as jnp
from jax import lax

F = 256
TILE = 128
BLK_DEV = 2
WORDS = 16
TMAX = 64
NODES = 8192
N_ROW = 4
N_COL = 8


def draw_tiles(key, part):
    key = jax.random.fold_in(key, 11)
    block_rows = N_COL * BLK_DEV
    block_cols = N_ROW * BLK_DEV
    keys = jax.random.split(key, N_ROW * N_COL)

    def one_device(device_key):
        position = jax.random.permutation(device_key, block_rows * block_cols)[:TMAX].astype(jnp.int32)
        return jnp.stack([position // block_cols, position % block_cols])
    return jax.vmap(one_device)(keys).reshape(N_ROW, N_COL, 2, TMAX).astype(jnp.int32)


def draw_tile_count(key, part):
    key = jax.random.fold_in(key, 23)
    first_key, second_key = jax.random.split(key)
    counts = jax.random.randint(first_key, (N_ROW * N_COL,), TMAX // 8, TMAX // 2 + 1)
    busiest = jax.random.randint(second_key, (), 0, N_ROW * N_COL)
    counts = jnp.where(jnp.arange(N_ROW * N_COL) == busiest, TMAX, counts)
    return counts.reshape(N_ROW, N_COL).astype(jnp.int32)


def set_ends(values, stream_key, least, top_value):
    longest = values.shape.index(max(values.shape))
    spots = []
    for shift in (0, 1):
        where = [jax.random.randint(jax.random.fold_in(stream_key, axis), (), 0, length) for axis, length in enumerate(values.shape)]
        where[longest] = (where[longest] + shift) % values.shape[longest]
        spots.append(tuple(where))
    return values.at[spots[0]].set(least).at[spots[1]].set(top_value)


def steps_of(key, shape, cuts, least, high):
    level = 1.0
    for axis_at, parts in cuts:
        draws = jax.random.uniform(jax.random.fold_in(jax.random.fold_in(key, 6), axis_at), (parts,), jnp.float32, least / len(cuts), high / len(cuts))
        level = level * jnp.repeat(jnp.exp(draws), shape[axis_at] // parts).reshape((-1,) + (1,) * (len(shape) - 1 - axis_at))
    return level


def scatter_about(rng, shape, width, bound, cuts=(), kind=jnp.bfloat16):
    values = width * jax.random.normal(rng, shape, jnp.float32)
    if cuts:
        values = values * steps_of(rng, shape, cuts, -0.22, 0.18)
    return jnp.clip(values, -bound, bound).astype(kind)


def setup_inputs(seed: int = 0) -> dict:
    seeds = jax.random.split(jax.random.key(seed), 7)
    return {
        "features": scatter_about(seeds[0], (NODES, F), 1.0, 6.0, ((0, 32),)),
        "weight": scatter_about(seeds[1], (F, F), F ** -0.5, 0.375),
        "cotangent": scatter_about(seeds[2], (NODES, F), 1.0, 6.0, ((0, 32),)),
        "tiles": draw_tiles(jax.random.fold_in(seeds[6], 71), 0),
        "tile_count": draw_tile_count(jax.random.fold_in(seeds[6], 71), 0),
        "patterns": set_ends(jax.random.randint(seeds[5], (N_ROW, N_COL, TMAX, WORDS, TILE), 0, 256), jax.random.fold_in(seeds[5], 1), 0, 255).astype(jnp.int32),
    }


def unpack(packed):
    shifts = jnp.arange(8, dtype=jnp.int32)
    bits = jnp.bitwise_and(jnp.right_shift(packed[:, :, None, :], shifts[:, None]), 1)
    return bits.reshape(packed.shape[0], packed.shape[1] * 8, packed.shape[2])

def rounded(value):
    narrow = lax.optimization_barrier(value.astype(jnp.bfloat16))
    return narrow.astype(jnp.float32)

def reference(features, weight, cotangent, tiles, tile_count, patterns):
    rows_dev = TILE * BLK_DEV
    nodes = rows_dev * N_ROW * N_COL
    offsets = jnp.arange(TILE, dtype=jnp.int32)
    feats_wide = features.astype(jnp.float32)

    def locate(device):
        row_pos = device // N_COL
        col_pos = device % N_COL
        row_first = row_pos * N_COL * rows_dev + tiles[row_pos, col_pos, 0] * TILE
        block_col = tiles[row_pos, col_pos, 1]
        col_first = (block_col // BLK_DEV * N_COL + col_pos) * rows_dev + block_col % BLK_DEV * TILE
        live = (jnp.arange(TMAX, dtype=jnp.int32) < tile_count[row_pos, col_pos]).astype(jnp.float32)
        pattern = unpack(patterns[row_pos, col_pos]).astype(jnp.float32) * live[:, None, None]
        rows = (row_first[:, None] + offsets[None, :]).astype(jnp.int32)
        cols = (col_first[:, None] + offsets[None, :]).astype(jnp.int32)
        return (rows, cols, pattern)

    def forward(carry, device):
        summed, degree = carry
        rows, cols, pattern = locate(device)
        product = jnp.einsum('tki,tkf->tif', pattern, feats_wide[cols])
        part_sum = jnp.zeros((nodes, F), jnp.float32).at[rows].add(product)
        part_degree = jnp.zeros((nodes,), jnp.float32).at[rows].add(lax.optimization_barrier(jnp.sum(pattern, axis=1)))
        return ((summed + rounded(part_sum), degree + rounded(part_degree)), None)
    devices = jnp.arange(N_ROW * N_COL, dtype=jnp.int32)
    start = (jnp.zeros((nodes, F), jnp.float32), jnp.zeros((nodes,), jnp.float32))
    (summed, degree), _ = lax.scan(forward, start, devices)
    scale = lax.rsqrt(degree + 1.0)
    aggregated = (summed * scale[:, None] + feats_wide).astype(jnp.bfloat16)
    preact = jnp.dot(aggregated, weight, preferred_element_type=jnp.float32)
    gate_value = jax.nn.sigmoid(preact)
    activated = (preact * gate_value).astype(jnp.bfloat16)
    grad_preact = (cotangent.astype(jnp.float32) * gate_value * (1.0 + preact * (1.0 - gate_value))).astype(jnp.bfloat16)
    grad_weight = lax.dot_general(aggregated, grad_preact, (((0,), (0,)), ((), ())), preferred_element_type=jnp.float32)
    grad_aggregated = lax.dot_general(grad_preact, weight, (((1,), (1,)), ((), ())), preferred_element_type=jnp.float32)
    grad_scaled = (grad_aggregated * scale[:, None]).astype(jnp.bfloat16)
    scaled_wide = grad_scaled.astype(jnp.float32)

    def backward(back, device):
        rows, cols, pattern = locate(device)
        product = jnp.einsum('tki,tif->tkf', pattern, scaled_wide[rows])
        part_back = jnp.zeros((nodes, F), jnp.float32).at[cols].add(product)
        return (back + rounded(part_back), None)
    back, _ = lax.scan(backward, jnp.zeros((nodes, F), jnp.float32), devices)
    grad_features = (back + grad_aggregated).astype(jnp.bfloat16)
    return (activated, grad_features, grad_weight)
```

```python
import functools

import jax
import jax.numpy as jnp
from jax import lax
from jax.experimental import pallas as pl
from jax.experimental.pallas import tpu as pltpu
from jax.sharding import PartitionSpec as P

VMEM_LIMIT = 56 * 1024 * 1024
pad_rows = 16


def vmem(count):
    return [pl.BlockSpec(memory_space=pltpu.VMEM)] * count


def smem(count):
    return [pl.BlockSpec(memory_space=pltpu.SMEM)] * count


def params():
    return pltpu.CompilerParams(vmem_limit_bytes=VMEM_LIMIT)


def cost(flops, nbytes):
    return pl.CostEstimate(flops=int(flops), bytes_accessed=int(nbytes), transcendentals=0)


def clear(ref):
    rows, width = ref.shape
    step = 128
    zeros = jnp.zeros((step, width), ref.dtype)

    def body(i, _):
        ref[pl.ds(pl.multiple_of(i * step, step), step), :] = zeros
        return 0

    lax.fori_loop(0, rows // step, body, 0)


def unpack_tile(words):
    groups, tile = words.shape
    wide = jnp.broadcast_to(words[:, None, :], (groups, 8, tile))
    shifts = lax.broadcasted_iota(jnp.int32, (groups, 8, tile), 1)
    bits = jnp.bitwise_and(jnp.right_shift(wide, shifts), 1)
    return bits.reshape(groups * 8, tile).astype(jnp.float32).astype(jnp.bfloat16)


def build_forward(blocks, tiles, count, patterns, tiles2, count2, patterns2, st_ref, degree_ref):
    my_row = lax.axis_index("row")
    my_col = lax.axis_index("col")
    my_z, core = my_col // 2, my_col % 2
    tile = patterns.shape[-1]
    half = st_ref.shape[0] // 2
    clear(st_ref)

    def add(tiles_ref, patterns_ref, first):
        def step(t, _):
            a, b = tiles_ref[0, t], tiles_ref[1, t]
            dest = a // blocks

            @pl.when(dest % 2 == core)
            def _():
                i0 = (((dest // 2) ^ my_z) * blocks + a % blocks) * tile
                k0 = first + (((b // blocks) ^ my_row) * blocks + b % blocks) * tile
                st_ref[pl.ds(pl.multiple_of(k0, tile), tile), pl.ds(pl.multiple_of(i0, tile), tile)] = unpack_tile(
                    patterns_ref[t]
                )

            return 0

        return step

    lax.fori_loop(0, count[0, 0], add(tiles, patterns, 0), 0)
    lax.fori_loop(0, count2[0, 0], add(tiles2, patterns2, half), 0)
    ones = jnp.ones((pad_rows, st_ref.shape[0]), jnp.bfloat16)
    degree = jnp.dot(ones, st_ref[...], preferred_element_type=jnp.float32)
    high = jnp.floor(degree * (1.0 / 64.0)) * 64.0
    line = lax.broadcasted_iota(jnp.int32, degree.shape, 0)
    degree_ref[...] = jnp.where(line == 0, high, jnp.where(line == 1, degree - high, 0.0)).astype(jnp.bfloat16)


def build_backward(blocks, n_z, tiles, count, patterns, st_ref):
    my_row = lax.axis_index("row")
    my_col = lax.axis_index("col")
    my_z, core = my_col // 2, my_col % 2
    tile = patterns.shape[-1]
    clear(st_ref)

    def step(t, _):
        a, b = tiles[0, t], tiles[1, t]
        dest = a // blocks
        i0 = ((((dest % 2) ^ core) * n_z + ((dest // 2) ^ my_z)) * blocks + a % blocks) * tile
        k0 = (((b // blocks) ^ my_row) * blocks + b % blocks) * tile
        st_ref[pl.ds(pl.multiple_of(k0, tile), tile), pl.ds(pl.multiple_of(i0, tile), tile)] = unpack_tile(patterns[t])
        return 0

    lax.fori_loop(0, count[0, 0], step, 0)


def forward_kernel(n_feats, n_z, *refs):
    feats, st_ref, degree_ref, outs, feats_t = (
        refs[:n_feats],
        refs[n_feats],
        refs[n_feats + 1],
        refs[n_feats + 2 : n_feats + 2 + n_z],
        refs[-1],
    )
    rows, width = feats[0].shape
    for i, ref in enumerate(feats):
        feats_t[:, i * rows : (i + 1) * rows] = ref[...].T
    for j, out in enumerate(outs):
        columns = slice(j * rows, (j + 1) * rows)
        out[:width, :] = jnp.dot(
            feats_t[...], st_ref[:, columns], preferred_element_type=jnp.float32
        ).astype(jnp.bfloat16)
        out[width:, :] = degree_ref[:, columns]


def dense_kernel(n_z, *refs):
    parts = refs[:n_z]
    feats, cotangent, weight = refs[n_z : n_z + 3]
    act_ref, scaled_ref, agg_grad_ref, keep_ref, send_ref = refs[n_z + 3 :]
    width = weight.shape[0]
    core = lax.axis_index("col") % 2
    total = parts[0][...].astype(jnp.float32)
    for part in parts[1:]:
        total = total + part[...].astype(jnp.float32)
    degree = total[width : width + 1] + total[width + 1 : width + 2]
    scale = lax.rsqrt(degree + 1.0)
    agg_t = (total[:width] * scale + feats[...].astype(jnp.float32).T).astype(jnp.bfloat16)
    agg = agg_t.T
    w = weight[...]
    preact = jnp.dot(agg, w, preferred_element_type=jnp.float32)
    gate = jax.nn.sigmoid(preact)
    act_ref[...] = (preact * gate).astype(jnp.bfloat16)
    grad_pre = (cotangent[...].astype(jnp.float32) * gate * (1.0 + preact * (1.0 - gate))).astype(jnp.bfloat16)
    grad_agg = lax.dot_general(grad_pre, w, (((1,), (1,)), ((), ())), preferred_element_type=jnp.float32)
    agg_grad_ref[...] = grad_agg
    scale_rows = jnp.broadcast_to(scale, agg_t.shape).T
    scaled_ref[...] = (grad_agg * scale_rows).astype(jnp.bfloat16)
    part = jnp.dot(agg_t, grad_pre, preferred_element_type=jnp.float32).astype(jnp.bfloat16)
    half = width // 2
    low, high = part[:half], part[half:]
    first = core == 0
    keep_ref[...] = jnp.where(first, low, high)
    send_ref[...] = jnp.where(first, high, low)


def backward_kernel(n_grads, n_row, *refs):
    st_ref, grads, outs = refs[0], refs[1 : 1 + n_grads], refs[1 + n_grads : 1 + n_grads + n_row]
    gathered = refs[-1]
    rows, _ = grads[0].shape
    for i, ref in enumerate(grads):
        gathered[i * rows : (i + 1) * rows, :] = ref[...]
    for j, out in enumerate(outs):
        out[...] = jnp.dot(
            st_ref[j * rows : (j + 1) * rows, :], gathered[...], preferred_element_type=jnp.float32
        ).astype(out.dtype)


def weight_kernel(n_z, mine, other, out_ref):
    my_col = lax.axis_index("col")
    my_z, core = my_col // 2, my_col % 2
    piece = mine.shape[0] // n_z
    half = out_ref.shape[0] // 2
    for flip, ref in enumerate((mine, other)):
        for j in range(n_z):
            at = (core ^ flip) * half + (my_z ^ j) * piece
            out_ref[pl.ds(pl.multiple_of(at, piece), piece), :] = ref[j * piece : (j + 1) * piece, :].astype(
                out_ref.dtype
            )


def tree_sum(values):
    while len(values) > 1:
        values = [values[i] + values[i + 1] for i in range(0, len(values), 2)]
    return values[0]


def per_device(features, weight, cotangent, tiles, tile_count, patterns):
    rows, width = features.shape
    slots, words, tile = patterns.shape[2:]
    blocks = rows // tile
    n_row = lax.axis_size("row")
    n_col = lax.axis_size("col")
    n_z = n_col // 2
    my_z = lax.axis_index("col") // 2
    row_len = n_z * rows
    col_len = n_row * rows
    bf16, f32 = jnp.bfloat16, jnp.float32
    shape = jax.ShapeDtypeStruct

    def over_row(x, k):
        return lax.ppermute(x, "row", [(i, i ^ k) for i in range(n_row)])

    def over_z(x, k):
        return lax.ppermute(x, "col", [(i, i ^ (2 * k)) for i in range(n_col)])

    def over_core(x):
        return lax.ppermute(x, "col", [(i, i ^ 1) for i in range(n_col)])

    tiles, patterns = tiles[0, 0], patterns[0, 0]
    patterns2, tiles2, count2 = over_core(patterns), over_core(tiles), over_core(tile_count)

    feats = [features] + [over_row(features, k) for k in range(1, n_row)]
    feats = feats + [over_core(x) for x in feats]

    st_forward, degree = pl.pallas_call(
        functools.partial(build_forward, blocks),
        out_shape=(shape((2 * col_len, row_len), bf16), shape((pad_rows, row_len), bf16)),
        in_specs=smem(2) + vmem(1) + smem(2) + vmem(1),
        out_specs=tuple(vmem(2)),
        compiler_params=params(),
        cost_estimate=cost(2e9, 8e6),
        name="build_forward",
    )(tiles, tile_count, patterns, tiles2, count2, patterns2)

    parts = pl.pallas_call(
        functools.partial(forward_kernel, len(feats), n_z),
        out_shape=[shape((width + pad_rows, rows), bf16)] * n_z,
        in_specs=vmem(len(feats) + 2),
        out_specs=vmem(n_z),
        scratch_shapes=[pltpu.VMEM((width, 2 * col_len), bf16)],
        compiler_params=params(),
        cost_estimate=cost(2 * width * 2 * col_len * row_len, 6e6),
        name="forward",
    )(*feats, st_forward, degree)
    parts = [parts[0]] + [over_z(parts[k], k) for k in range(1, n_z)]

    st_backward = pl.pallas_call(
        functools.partial(build_backward, blocks, n_z),
        out_shape=shape((col_len, 2 * row_len), bf16),
        in_specs=smem(2) + vmem(1),
        out_specs=vmem(1)[0],
        compiler_params=params(),
        cost_estimate=cost(2e9, 8e6),
        name="build_backward",
    )(tiles, tile_count, patterns)

    activated, scaled, grad_agg, keep, send = pl.pallas_call(
        functools.partial(dense_kernel, n_z),
        out_shape=(
            shape((rows, width), bf16),
            shape((rows, width), bf16),
            shape((rows, width), f32),
            shape((width // 2, width), bf16),
            shape((width // 2, width), bf16),
        ),
        in_specs=vmem(n_z + 3),
        out_specs=tuple(vmem(5)),
        compiler_params=params(),
        cost_estimate=cost(6 * rows * width * width, 2e6),
        name="dense",
    )(*parts, features, cotangent, weight)

    grads = [scaled] + [over_z(scaled, k) for k in range(1, n_z)]
    grads = grads + [over_core(x) for x in grads]

    half = keep.astype(f32) + over_core(send).astype(f32)
    piece = width // 2 // n_z
    cut = [lax.dynamic_slice_in_dim(half, (my_z ^ k) * piece, piece, 0).astype(bf16) for k in range(n_z)]
    got = [cut[0]] + [over_z(cut[k], k) for k in range(1, n_z)]
    got = tree_sum([x.astype(f32) for x in got]).astype(bf16)
    got = [got] + [over_row(got, k) for k in range(1, n_row)]
    got = tree_sum([x.astype(f32) for x in got]).astype(bf16)
    mine = jnp.concatenate([got] + [over_z(got, k) for k in range(1, n_z)], axis=0)
    other = over_core(mine)
    grad_weight = pl.pallas_call(
        functools.partial(weight_kernel, n_z),
        out_shape=shape((width, width), f32),
        in_specs=vmem(2),
        out_specs=vmem(1)[0],
        compiler_params=params(),
        cost_estimate=cost(1e6, 4e5),
        name="weight_out",
    )(mine, other)

    backs = pl.pallas_call(
        functools.partial(backward_kernel, len(grads), n_row),
        out_shape=[shape((rows, width), bf16)] * n_row,
        in_specs=vmem(1 + len(grads)),
        out_specs=vmem(n_row),
        scratch_shapes=[pltpu.VMEM((2 * row_len, width), bf16)],
        compiler_params=params(),
        cost_estimate=cost(2 * width * 2 * col_len * row_len, 6e6),
        name="backward",
    )(st_backward, *grads)
    backs = [backs[0]] + [over_row(backs[k], k) for k in range(1, n_row)]
    grad_features = (tree_sum([x.astype(f32) for x in backs]) + grad_agg).astype(bf16)
    return activated, grad_features, grad_weight


def solution(mesh):
    return jax.shard_map(
        per_device,
        mesh=mesh,
        in_specs=(
            P(("row", "col"), None),
            P(),
            P(("row", "col"), None),
            P("row", "col", None, None),
            P("row", "col"),
            P("row", "col", None, None, None),
        ),
        out_specs=(P(("row", "col"), None), P(("row", "col"), None), P()),
        check_vma=False,
    )
```

```python
import functools
import math

import jax
import jax.numpy as jnp
from jax import lax
from jax.experimental import pallas as pl
from jax.experimental.pallas import tpu as pltpu
from jax.sharding import PartitionSpec as P

pad_rows = 16
resident_bytes = 9 << 20
bf16, f32 = jnp.bfloat16, jnp.float32


def fits(shape, dtype):
    return math.prod(shape) * jnp.dtype(dtype).itemsize <= resident_bytes


def smem(count):
    return [pl.BlockSpec(memory_space=pltpu.SMEM)] * count


def call(body, name, outs, args, n_smem=0, scratch=(), limit=24, flops=1e6, final=()):
    kept = [
        x if i < n_smem or not fits(x.shape, x.dtype) else pltpu.with_memory_space_constraint(x, pltpu.VMEM)
        for i, x in enumerate(args)
    ]
    shapes = [
        pltpu.VMEM(shape, dtype) if i not in final and fits(shape, dtype) else jax.ShapeDtypeStruct(shape, dtype)
        for i, (shape, dtype) in enumerate(outs)
    ]
    vmem = pl.BlockSpec(memory_space=pltpu.VMEM)
    large = any(not fits(x.shape, x.dtype) for x in args) or any(not fits(*out) for out in outs)
    return pl.pallas_call(
        body,
        out_shape=shapes,
        in_specs=smem(n_smem) + [vmem] * (len(args) - n_smem),
        out_specs=[vmem] * len(outs),
        scratch_shapes=scratch,
        compiler_params=pltpu.CompilerParams(vmem_limit_bytes=(48 if large else limit) << 20),
        cost_estimate=pl.CostEstimate(flops=int(flops), bytes_accessed=1 << 20, transcendentals=0),
        name=name,
    )(*kept)


def clear(ref):
    rows, width = ref.shape
    step = 128
    zeros = jnp.zeros((step, width), ref.dtype)

    def body(i, _):
        ref[pl.ds(pl.multiple_of(i * step, step), step), :] = zeros
        return 0

    lax.fori_loop(0, rows // step, body, 0)


def unpack_tile(words):
    groups, tile = words.shape
    wide = jnp.broadcast_to(words[:, None, :], (groups, 8, tile))
    shifts = lax.broadcasted_iota(jnp.int32, (groups, 8, tile), 1)
    bits = jnp.bitwise_and(jnp.right_shift(wide, shifts), 1)
    return bits.reshape(groups * 8, tile).astype(jnp.float32).astype(jnp.bfloat16)


def build_forward(blocks, meta, meta2, patterns, patterns2, st_ref):
    my_row = lax.axis_index("row")
    my_col = lax.axis_index("col")
    my_z, core = my_col // 2, my_col % 2
    tile = patterns.shape[-1]
    half = st_ref.shape[0] // 2
    clear(st_ref)

    def add(meta_ref, patterns_ref, first):
        def step(t, _):
            a, b = meta_ref[0, t], meta_ref[1, t]
            dest = a // blocks

            @pl.when(dest % 2 == core)
            def _():
                i0 = (((dest // 2) ^ my_z) * blocks + a % blocks) * tile
                k0 = first + (((b // blocks) ^ my_row) * blocks + b % blocks) * tile
                st_ref[pl.ds(pl.multiple_of(k0, tile), tile), pl.ds(pl.multiple_of(i0, tile), tile)] = unpack_tile(
                    patterns_ref[t]
                )

            return 0

        return step

    lax.fori_loop(0, meta[2, 0], add(meta, patterns, 0), 0)
    lax.fori_loop(0, meta2[2, 0], add(meta2, patterns2, half), 0)


def build_backward(blocks, n_z, meta, patterns, st_ref):
    my_row = lax.axis_index("row")
    my_col = lax.axis_index("col")
    my_z, core = my_col // 2, my_col % 2
    tile = patterns.shape[-1]
    clear(st_ref)

    def step(t, _):
        a, b = meta[0, t], meta[1, t]
        dest = a // blocks
        i0 = ((((dest % 2) ^ core) * n_z + ((dest // 2) ^ my_z)) * blocks + a % blocks) * tile
        k0 = (((b // blocks) ^ my_row) * blocks + b % blocks) * tile
        st_ref[pl.ds(pl.multiple_of(k0, tile), tile), pl.ds(pl.multiple_of(i0, tile), tile)] = unpack_tile(patterns[t])
        return 0

    lax.fori_loop(0, meta[2, 0], step, 0)


def forward_kernel(n_feats, n_z, *refs):
    st_ref, feats, outs, feats_t = refs[0], refs[1 : 1 + n_feats], refs[1 + n_feats : 1 + n_feats + n_z], refs[-1]
    rows, width = feats[0].shape
    for i, ref in enumerate(feats):
        feats_t[:width, i * rows : (i + 1) * rows] = ref[...].T
    feats_t[width:, :] = jnp.ones((pad_rows, feats_t.shape[1]), bf16)
    line = lax.broadcasted_iota(jnp.int32, (pad_rows, rows), 0)
    for j, out in enumerate(outs):
        product = jnp.dot(feats_t[...], st_ref[:, j * rows : (j + 1) * rows], preferred_element_type=f32)
        out[:width, :] = product[:width].astype(bf16)
        degree = product[width:]
        high = jnp.floor(degree * (1.0 / 64.0)) * 64.0
        out[width:, :] = jnp.where(line == 0, high, jnp.where(line == 1, degree - high, 0.0)).astype(bf16)


def dense_kernel(n_z, *refs):
    parts = refs[:n_z]
    feats, cotangent, weight = refs[n_z : n_z + 3]
    act_ref, scaled_ref, agg_grad_ref, agg_ref, grad_ref = refs[n_z + 3 :]
    width = weight.shape[0]
    total = parts[0][...].astype(f32)
    for part in parts[1:]:
        total = total + part[...].astype(f32)
    degree = total[width : width + 1] + total[width + 1 : width + 2]
    scale = lax.rsqrt(degree + 1.0)
    agg_t = (total[:width] * scale + feats[...].astype(f32).T).astype(bf16)
    agg_ref[...] = agg_t
    w = weight[...]
    preact = jnp.dot(agg_t.T, w, preferred_element_type=f32)
    gate = jax.nn.sigmoid(preact)
    act_ref[...] = (preact * gate).astype(bf16)
    grad_pre = (cotangent[...].astype(f32) * gate * (1.0 + preact * (1.0 - gate))).astype(bf16)
    grad_ref[...] = grad_pre
    grad_agg = lax.dot_general(grad_pre, w, (((1,), (1,)), ((), ())), preferred_element_type=f32)
    agg_grad_ref[...] = grad_agg
    scale_rows = jnp.broadcast_to(scale, agg_t.shape).T
    scaled_ref[...] = (grad_agg * scale_rows).astype(bf16)


def weight_kernel(agg_t, grad_pre, keep_ref, send_ref):
    first = lax.axis_index("col") % 2 == 0
    half = agg_t.shape[0] // 2
    part = jnp.dot(agg_t[...], grad_pre[...], preferred_element_type=f32).astype(bf16)
    keep_ref[...] = jnp.where(first, part[:half], part[half:])
    send_ref[...] = jnp.where(first, part[half:], part[:half])


def backward_kernel(n_grads, n_row, *refs):
    st_ref, grads, outs = refs[0], refs[1 : 1 + n_grads], refs[1 + n_grads : 1 + n_grads + n_row]
    gathered = refs[-1]
    rows, _ = grads[0].shape
    for i, ref in enumerate(grads):
        gathered[i * rows : (i + 1) * rows, :] = ref[...]
    for j, out in enumerate(outs):
        out[...] = jnp.dot(st_ref[j * rows : (j + 1) * rows, :], gathered[...], preferred_element_type=f32).astype(
            out.dtype
        )


def tree_sum(values):
    values = [x.astype(f32) for x in values]
    while len(values) > 1:
        values = [values[i] + values[i + 1] for i in range(0, len(values), 2)]
    return values[0]


def per_device(features, weight, cotangent, tiles, tile_count, patterns):
    rows, width = features.shape
    slots, words, tile = patterns.shape[2:]
    blocks = rows // tile
    n_row = lax.axis_size("row")
    n_col = lax.axis_size("col")
    n_z = n_col // 2
    core = lax.axis_index("col") % 2
    row_len = n_z * rows
    col_len = n_row * rows
    flops = 4 * width * col_len * row_len

    def over_row(x, k):
        return lax.ppermute(x, "row", [(i, i ^ k) for i in range(n_row)])

    def over_z(x, k):
        return lax.ppermute(x, "col", [(i, i ^ (2 * k)) for i in range(n_col)])

    def over_core(x):
        return lax.ppermute(x, "col", [(i, i ^ 1) for i in range(n_col)])

    patterns = patterns[0, 0]
    meta = jnp.concatenate([tiles[0, 0], jnp.broadcast_to(tile_count, (1, slots))], axis=0)
    patterns2, meta2 = over_core(patterns), over_core(meta)
    feats = [features] + [over_row(features, k) for k in range(1, n_row)]

    (st_forward,) = call(
        functools.partial(build_forward, blocks),
        "build_forward",
        [((2 * col_len, row_len), bf16)],
        [meta, meta2, patterns, patterns2],
        n_smem=2,
        flops=2e9,
    )
    feats, st_forward = lax.optimization_barrier((feats, st_forward))
    feats = feats + [over_core(x) for x in feats]

    parts = call(
        functools.partial(forward_kernel, len(feats), n_z),
        "forward",
        [((width + pad_rows, rows), bf16)] * n_z,
        [st_forward] + feats,
        scratch=[pltpu.VMEM((width + pad_rows, 2 * col_len), bf16)],
        flops=flops,
    )
    travelling = [over_z(parts[k], k) for k in range(1, n_z)]
    (st_backward,) = call(
        functools.partial(build_backward, blocks, n_z),
        "build_backward",
        [((col_len, 2 * row_len), bf16)],
        [meta, patterns],
        n_smem=1,
        flops=2e9,
    )
    own, travelling, st_backward = lax.optimization_barrier((parts[0], travelling, st_backward))

    activated, scaled, grad_agg, agg_t, grad_pre = call(
        functools.partial(dense_kernel, n_z),
        "dense",
        [((rows, width), bf16), ((rows, width), bf16), ((rows, width), f32), ((width, rows), bf16), ((rows, width), bf16)],
        [own] + travelling + [features, cotangent, weight],
        flops=4 * rows * width * width,
        final=(0,),
    )
    grads = [scaled] + [over_z(scaled, k) for k in range(1, n_z)]
    grads = grads + [over_core(x) for x in grads]

    keep, send = call(
        weight_kernel,
        "weight_part",
        [((width // 2, width), bf16)] * 2,
        [agg_t, grad_pre],
        flops=2e9,
    )
    half = (keep.astype(f32) + over_core(send).astype(f32)).astype(bf16)
    half = tree_sum([half] + [over_row(half, k) for k in range(1, n_row)]).astype(bf16)
    half = tree_sum([half] + [over_z(half, k) for k in range(1, n_z)])
    other = over_core(half)
    grad_weight = jnp.concatenate([jnp.where(core == 0, half, other), jnp.where(core == 0, other, half)], axis=0)

    backs = call(
        functools.partial(backward_kernel, len(grads), n_row),
        "backward",
        [((rows, width), bf16)] * n_row,
        [st_backward] + grads,
        scratch=[pltpu.VMEM((2 * row_len, width), bf16)],
        flops=flops,
    )
    backs = [backs[0]] + [over_row(backs[k], k) for k in range(1, n_row)]
    grad_features = (tree_sum(backs) + grad_agg).astype(bf16)
    return activated, grad_features, grad_weight


def solution(mesh):
    return jax.shard_map(
        per_device,
        mesh=mesh,
        in_specs=(
            P(("row", "col"), None),
            P(),
            P(("row", "col"), None),
            P("row", "col", None, None),
            P("row", "col"),
            P("row", "col", None, None, None),
        ),
        out_specs=(P(("row", "col"), None), P(("row", "col"), None), P()),
        check_vma=False,
    )
```

```python
import functools
import math

import jax
import jax.numpy as jnp
from jax import lax
from jax.experimental import pallas as pl
from jax.experimental.pallas import tpu as pltpu
from jax.sharding import PartitionSpec as P

pad_rows = 16
resident_bytes = 9 << 20
bf16, f32 = jnp.bfloat16, jnp.float32


def fits(shape, dtype):
    return math.prod(shape) * jnp.dtype(dtype).itemsize <= resident_bytes


def smem(count):
    return [pl.BlockSpec(memory_space=pltpu.SMEM)] * count


def call(body, name, outs, args, n_smem=0, anywhere=(), scratch=(), limit=8, flops=1e6, final=()):
    kept = [
        x if i < n_smem or i in anywhere or not fits(x.shape, x.dtype) else pltpu.with_memory_space_constraint(x, pltpu.VMEM)
        for i, x in enumerate(args)
    ]
    shapes = [
        pltpu.VMEM(shape, dtype) if i not in final and fits(shape, dtype) else jax.ShapeDtypeStruct(shape, dtype)
        for i, (shape, dtype) in enumerate(outs)
    ]
    vmem = pl.BlockSpec(memory_space=pltpu.VMEM)
    large = any(not fits(x.shape, x.dtype) for x in args) or any(not fits(*out) for out in outs)
    return pl.pallas_call(
        body,
        out_shape=shapes,
        in_specs=smem(n_smem)
        + [pl.BlockSpec(memory_space=pl.ANY) if i in anywhere else vmem for i in range(n_smem, len(args))],
        out_specs=[vmem] * len(outs),
        scratch_shapes=scratch,
        compiler_params=pltpu.CompilerParams(vmem_limit_bytes=(48 if large else limit) << 20),
        cost_estimate=pl.CostEstimate(flops=int(flops), bytes_accessed=1 << 20, transcendentals=0),
        name=name,
    )(*kept)


def clear(ref):
    rows, width = ref.shape
    step = 128
    zeros = jnp.zeros((step, width), ref.dtype)

    def body(i, _):
        ref[pl.ds(pl.multiple_of(i * step, step), step), :] = zeros
        return 0

    lax.fori_loop(0, rows // step, body, 0)


def unpack_tile(words):
    groups, tile = words.shape
    wide = jnp.broadcast_to(words[:, None, :], (groups, 8, tile))
    shifts = lax.broadcasted_iota(jnp.int32, (groups, 8, tile), 1)
    bits = jnp.bitwise_and(jnp.right_shift(wide, shifts), 1)
    return bits.reshape(groups * 8, tile).astype(jnp.float32).astype(jnp.bfloat16)


def build_kernel(blocks, n_z, tiles, count, patterns, st_ref, held, sem):
    my_row = lax.axis_index("row")
    my_col = lax.axis_index("col")
    my_z, core = my_col // 2, my_col % 2
    tile = patterns.shape[-1]
    copy = pltpu.make_async_copy(patterns, held, sem)
    copy.start()
    clear(st_ref)
    copy.wait()

    def step(t, _):
        a, b = tiles[0, t], tiles[1, t]
        dest = a // blocks
        i0 = ((((dest % 2) ^ core) * n_z + ((dest // 2) ^ my_z)) * blocks + a % blocks) * tile
        k0 = (((b // blocks) ^ my_row) * blocks + b % blocks) * tile
        st_ref[pl.ds(pl.multiple_of(k0, tile), tile), pl.ds(pl.multiple_of(i0, tile), tile)] = unpack_tile(held[t])
        return 0

    lax.fori_loop(0, count[0, 0], step, 0)


def forward_block(feats_t, st_ref, first, rows, width):
    line = lax.broadcasted_iota(jnp.int32, (pad_rows, rows), 0)
    product = jnp.dot(feats_t[...], st_ref[:, first : first + rows], preferred_element_type=f32)
    degree = product[width:]
    high = jnp.floor(degree * (1.0 / 64.0)) * 64.0
    return product[:width].astype(bf16), jnp.where(line == 0, high, jnp.where(line == 1, degree - high, 0.0)).astype(bf16)


def forward_other(n_row, n_z, *refs):
    st_ref, feats, out, feats_t = refs[0], refs[1 : 1 + n_row], refs[-2], refs[-1]
    rows, width = feats[0].shape
    for i, ref in enumerate(feats):
        feats_t[:width, i * rows : (i + 1) * rows] = ref[...].T
    feats_t[width:, :] = jnp.ones((pad_rows, feats_t.shape[1]), bf16)
    for j in range(n_z):
        sums, degree = forward_block(feats_t, st_ref, (n_z + j) * rows, rows, width)
        out[j, :width, :] = sums
        out[j, width:, :] = degree


def forward_own(n_z, st_ref, feats_t, out):
    width, rows = out.shape[1] - pad_rows, out.shape[2]
    for j in range(n_z):
        sums, degree = forward_block(feats_t, st_ref, j * rows, rows, width)
        out[j, :width, :] = sums
        out[j, width:, :] = degree


def pair_kernel(own, other, *outs):
    for j, out in enumerate(outs):
        out[...] = (own[j].astype(f32) + other[j].astype(f32)).astype(bf16)


def dense_kernel(n_z, *refs):
    parts = refs[:n_z]
    feats, cotangent, weight = refs[n_z : n_z + 3]
    act_ref, scaled_ref, agg_grad_ref, agg_ref, grad_ref = refs[n_z + 3 :]
    width = weight.shape[0]
    total = parts[0][...].astype(f32)
    for part in parts[1:]:
        total = total + part[...].astype(f32)
    degree = total[width : width + 1] + total[width + 1 : width + 2]
    scale = lax.rsqrt(degree + 1.0)
    agg_t = (total[:width] * scale + feats[...].astype(f32).T).astype(bf16)
    agg_ref[...] = agg_t
    w = weight[...]
    preact = jnp.dot(agg_t.T, w, preferred_element_type=f32)
    gate = jax.nn.sigmoid(preact)
    act_ref[...] = (preact * gate).astype(bf16)
    grad_pre = (cotangent[...].astype(f32) * gate * (1.0 + preact * (1.0 - gate))).astype(bf16)
    grad_ref[...] = grad_pre
    grad_agg = lax.dot_general(grad_pre, w, (((1,), (1,)), ((), ())), preferred_element_type=f32)
    agg_grad_ref[...] = grad_agg
    scale_rows = jnp.broadcast_to(scale, agg_t.shape).T
    scaled_ref[...] = (grad_agg * scale_rows).astype(bf16)


def weight_kernel(agg_t, grad_pre, keep_ref, send_ref):
    first = lax.axis_index("col") % 2 == 0
    half = agg_t.shape[0] // 2
    part = jnp.dot(agg_t[...], grad_pre[...], preferred_element_type=f32).astype(bf16)
    keep_ref[...] = jnp.where(first, part[:half], part[half:])
    send_ref[...] = jnp.where(first, part[half:], part[:half])


def backward_kernel(n_grads, n_row, *refs):
    st_ref, grads, outs = refs[0], refs[1 : 1 + n_grads], refs[1 + n_grads : 1 + n_grads + n_row]
    gathered = refs[-1]
    rows, _ = grads[0].shape
    for i, ref in enumerate(grads):
        gathered[i * rows : (i + 1) * rows, :] = ref[...]
    for j, out in enumerate(outs):
        out[...] = jnp.dot(st_ref[j * rows : (j + 1) * rows, :], gathered[...], preferred_element_type=f32).astype(
            out.dtype
        )


def tree_sum(values):
    values = [x.astype(f32) for x in values]
    while len(values) > 1:
        values = [values[i] + values[i + 1] for i in range(0, len(values), 2)]
    return values[0]


def per_device(features, weight, cotangent, tiles, tile_count, patterns):
    rows, width = features.shape
    slots, words, tile = patterns.shape[2:]
    blocks = rows // tile
    n_row = lax.axis_size("row")
    n_col = lax.axis_size("col")
    n_z = n_col // 2
    core = lax.axis_index("col") % 2
    row_len = n_z * rows
    col_len = n_row * rows
    flops = 4 * width * col_len * row_len
    high = width + pad_rows

    def over_row(x, k):
        return lax.ppermute(x, "row", [(i, i ^ k) for i in range(n_row)])

    def over_z(x, k):
        return lax.ppermute(x, "col", [(i, i ^ (2 * k)) for i in range(n_col)])

    def over_core(x):
        return lax.ppermute(x, "col", [(i, i ^ 1) for i in range(n_col)])

    feats = [features] + [over_row(features, k) for k in range(1, n_row)]
    (st,) = call(
        functools.partial(build_kernel, blocks, n_z),
        "build",
        [((col_len, 2 * row_len), bf16)],
        [tiles[0, 0], tile_count, patterns[0, 0]],
        n_smem=2,
        anywhere=(2,),
        scratch=[pltpu.VMEM((slots, words, tile), jnp.int32), pltpu.SemaphoreType.DMA],
        flops=4e9,
    )

    sent, feats_t = call(
        functools.partial(forward_other, n_row, n_z),
        "forward_other",
        [((n_z, high, rows), bf16), ((high, col_len), bf16)],
        [st] + feats,
        flops=flops // 2,
    )
    (own,) = call(
        functools.partial(forward_own, n_z), "forward_own", [((n_z, high, rows), bf16)], [st, feats_t], flops=flops // 2
    )
    parts = call(pair_kernel, "pair_sum", [((high, rows), bf16)] * n_z, [own, over_core(sent)])
    parts = [parts[0]] + [over_z(parts[k], k) for k in range(1, n_z)]

    activated, scaled, grad_agg, agg_t, grad_pre = call(
        functools.partial(dense_kernel, n_z),
        "dense",
        [((rows, width), bf16), ((rows, width), bf16), ((rows, width), f32), ((width, rows), bf16), ((rows, width), bf16)],
        parts + [features, cotangent, weight],
        flops=4 * rows * width * width,
        final=(0,),
    )
    far = {k: over_z(scaled, k) for k in range(2, n_z)}

    keep, send = call(
        weight_kernel,
        "weight_part",
        [((width // 2, width), bf16)] * 2,
        [agg_t, grad_pre],
        flops=2e9,
    )
    half = (keep.astype(f32) + over_core(send).astype(f32)).astype(bf16)
    near, half = lax.optimization_barrier((scaled, half))
    grads = [scaled, over_z(near, 1)] + [far[k] for k in range(2, n_z)]
    grads = grads + [over_core(x) for x in grads]
    half = tree_sum([half] + [over_row(half, k) for k in range(1, n_row)]).astype(bf16)

    backs = call(
        functools.partial(backward_kernel, len(grads), n_row),
        "backward",
        [((rows, width), bf16)] * n_row,
        [st] + grads,
        scratch=[pltpu.VMEM((2 * row_len, width), bf16)],
        flops=flops,
    )
    backs, half = lax.optimization_barrier((backs, half))
    half = tree_sum([half] + [over_z(half, k) for k in range(1, n_z)])
    other = over_core(half)
    grad_weight = jnp.concatenate([jnp.where(core == 0, half, other), jnp.where(core == 0, other, half)], axis=0)

    backs = [backs[0]] + [over_row(backs[k], k) for k in range(1, n_row)]
    grad_features = (tree_sum(backs) + grad_agg).astype(bf16)
    return activated, grad_features, grad_weight


def solution(mesh):
    return jax.shard_map(
        per_device,
        mesh=mesh,
        in_specs=(
            P(("row", "col"), None),
            P(),
            P(("row", "col"), None),
            P("row", "col", None, None),
            P("row", "col"),
            P("row", "col", None, None, None),
        ),
        out_specs=(P(("row", "col"), None), P(("row", "col"), None), P()),
        check_vma=False,
    )
```

```python
import functools
import math

import jax
import jax.numpy as jnp
from jax import lax
from jax.experimental import pallas as pl
from jax.experimental.pallas import tpu as pltpu
from jax.sharding import PartitionSpec as P

pad_rows = 16
resident_bytes = 9 << 20
bf16, f32 = jnp.bfloat16, jnp.float32


def fits(shape, dtype):
    return math.prod(shape) * jnp.dtype(dtype).itemsize <= resident_bytes


def smem(count):
    return [pl.BlockSpec(memory_space=pltpu.SMEM)] * count


def call(body, name, outs, args, n_smem=0, anywhere=(), scratch=(), limit=8, flops=1e6, final=()):
    kept = [
        x if i < n_smem or i in anywhere or not fits(x.shape, x.dtype) else pltpu.with_memory_space_constraint(x, pltpu.VMEM)
        for i, x in enumerate(args)
    ]
    shapes = [
        pltpu.VMEM(shape, dtype) if i not in final and fits(shape, dtype) else jax.ShapeDtypeStruct(shape, dtype)
        for i, (shape, dtype) in enumerate(outs)
    ]
    vmem = pl.BlockSpec(memory_space=pltpu.VMEM)
    large = any(not fits(x.shape, x.dtype) for x in args) or any(not fits(*out) for out in outs)
    return pl.pallas_call(
        body,
        out_shape=shapes,
        in_specs=smem(n_smem)
        + [pl.BlockSpec(memory_space=pl.ANY) if i in anywhere else vmem for i in range(n_smem, len(args))],
        out_specs=[vmem] * len(outs),
        scratch_shapes=scratch,
        compiler_params=pltpu.CompilerParams(vmem_limit_bytes=(48 if large else limit) << 20),
        cost_estimate=pl.CostEstimate(flops=int(flops), bytes_accessed=1 << 20, transcendentals=0),
        name=name,
    )(*kept)


def clear(ref):
    rows, width = ref.shape
    step = 128
    zeros = jnp.zeros((step, width), ref.dtype)

    def body(i, _):
        ref[pl.ds(pl.multiple_of(i * step, step), step), :] = zeros
        return 0

    lax.fori_loop(0, rows // step, body, 0)


def unpack_tile(words):
    groups, tile = words.shape
    wide = jnp.broadcast_to(words[:, None, :], (groups, 8, tile))
    shifts = lax.broadcasted_iota(jnp.int32, (groups, 8, tile), 1)
    bits = jnp.bitwise_and(jnp.right_shift(wide, shifts), 1)
    return bits.reshape(groups * 8, tile).astype(jnp.float32).astype(jnp.bfloat16)


def build_kernel(blocks, n_z, tiles, count, patterns, st_ref, held, sem):
    my_row = lax.axis_index("row")
    my_col = lax.axis_index("col")
    my_z, core = my_col // 2, my_col % 2
    tile = patterns.shape[-1]
    copy = pltpu.make_async_copy(patterns, held, sem)
    copy.start()
    clear(st_ref)
    copy.wait()

    def step(t, _):
        a, b = tiles[0, t], tiles[1, t]
        dest = a // blocks
        i0 = ((((dest % 2) ^ core) * n_z + ((dest // 2) ^ my_z)) * blocks + a % blocks) * tile
        k0 = (((b // blocks) ^ my_row) * blocks + b % blocks) * tile
        st_ref[pl.ds(pl.multiple_of(k0, tile), tile), pl.ds(pl.multiple_of(i0, tile), tile)] = unpack_tile(held[t])
        return 0

    lax.fori_loop(0, count[0, 0], step, 0)


def forward_block(feats_t, st_ref, first, rows, width):
    line = lax.broadcasted_iota(jnp.int32, (pad_rows, rows), 0)
    product = jnp.dot(feats_t[...], st_ref[:, first : first + rows], preferred_element_type=f32)
    degree = product[width:]
    high = jnp.floor(degree * (1.0 / 64.0)) * 64.0
    return product[:width].astype(bf16), jnp.where(line == 0, high, jnp.where(line == 1, degree - high, 0.0)).astype(bf16)


def forward_first(n_row, start, *refs):
    st_ref, feats, out, feats_t = refs[0], refs[1 : 1 + n_row], refs[-2], refs[-1]
    rows, width = feats[0].shape
    for i, ref in enumerate(feats):
        feats_t[:width, i * rows : (i + 1) * rows] = ref[...].T
    feats_t[width:, :] = jnp.ones((pad_rows, feats_t.shape[1]), bf16)
    forward_more(start, st_ref, feats_t, out)


def forward_more(start, st_ref, feats_t, out):
    width, rows = out.shape[1] - pad_rows, out.shape[2]
    for j in range(out.shape[0]):
        sums, degree = forward_block(feats_t, st_ref, (start + j) * rows, rows, width)
        out[j, :width, :] = sums
        out[j, width:, :] = degree


def pair_kernel(own, other, *outs):
    for j, out in enumerate(outs):
        out[...] = (own[j].astype(f32) + other[j].astype(f32)).astype(bf16)


def dense_kernel(n_z, *refs):
    parts = refs[:n_z]
    feats, cotangent, weight = refs[n_z : n_z + 3]
    act_ref, scaled_ref, agg_grad_ref, agg_ref, grad_ref = refs[n_z + 3 :]
    width = weight.shape[0]
    total = parts[0][...].astype(f32)
    for part in parts[1:]:
        total = total + part[...].astype(f32)
    degree = total[width : width + 1] + total[width + 1 : width + 2]
    scale = lax.rsqrt(degree + 1.0)
    agg_t = (total[:width] * scale + feats[...].astype(f32).T).astype(bf16)
    agg_ref[...] = agg_t
    w = weight[...]
    preact = jnp.dot(agg_t.T, w, preferred_element_type=f32)
    gate = jax.nn.sigmoid(preact)
    act_ref[...] = (preact * gate).astype(bf16)
    grad_pre = (cotangent[...].astype(f32) * gate * (1.0 + preact * (1.0 - gate))).astype(bf16)
    grad_ref[...] = grad_pre
    grad_agg = lax.dot_general(grad_pre, w, (((1,), (1,)), ((), ())), preferred_element_type=f32)
    agg_grad_ref[...] = grad_agg
    scale_rows = jnp.broadcast_to(scale, agg_t.shape).T
    scaled_ref[...] = (grad_agg * scale_rows).astype(bf16)


def weight_kernel(agg_t, grad_pre, out_ref):
    out_ref[...] = jnp.dot(agg_t[...], grad_pre[...], preferred_element_type=f32).astype(bf16)


def backward_near(spots, *refs):
    st_ref, grads, out = refs[0], refs[1 : 1 + len(spots)], refs[1 + len(spots)]
    gathered = refs[-1]
    rows, _ = grads[0].shape
    for i, ref in enumerate(grads):
        gathered[i * rows : (i + 1) * rows, :] = ref[...]
    for j in range(out.shape[0] // rows):
        lines = slice(j * rows, (j + 1) * rows)
        columns = jnp.concatenate([st_ref[lines, k * rows : (k + 1) * rows] for k in spots], axis=1)
        out[lines, :] = jnp.dot(columns, gathered[...], preferred_element_type=f32)


def backward_far(spots, n_row, *refs):
    st_ref, near, grads, outs = refs[0], refs[1], refs[2 : 2 + len(spots)], refs[2 + len(spots) : 2 + len(spots) + n_row]
    gathered = refs[-1]
    rows, _ = grads[0].shape
    for i, ref in enumerate(grads):
        gathered[i * rows : (i + 1) * rows, :] = ref[...]
    for j, out in enumerate(outs):
        lines = slice(j * rows, (j + 1) * rows)
        columns = jnp.concatenate([st_ref[lines, k * rows : (k + 1) * rows] for k in spots], axis=1)
        out[...] = (near[lines, :] + jnp.dot(columns, gathered[...], preferred_element_type=f32)).astype(out.dtype)


def tree_sum(values):
    values = [x.astype(f32) for x in values]
    while len(values) > 1:
        values = [values[i] + values[i + 1] for i in range(0, len(values), 2)]
    return values[0]


def per_device(features, weight, cotangent, tiles, tile_count, patterns):
    rows, width = features.shape
    slots, words, tile = patterns.shape[2:]
    blocks = rows // tile
    n_row = lax.axis_size("row")
    n_col = lax.axis_size("col")
    n_z = n_col // 2
    row_len = n_z * rows
    col_len = n_row * rows
    flops = 4 * width * col_len * row_len
    high = width + pad_rows

    def over_row(x, k):
        return lax.ppermute(x, "row", [(i, i ^ k) for i in range(n_row)])

    def over_z(x, k):
        return lax.ppermute(x, "col", [(i, i ^ (2 * k)) for i in range(n_col)])

    def over_core(x):
        return lax.ppermute(x, "col", [(i, i ^ 1) for i in range(n_col)])

    feats = [features] + [over_row(features, k) for k in range(1, n_row)]
    (st,) = call(
        functools.partial(build_kernel, blocks, n_z),
        "build",
        [((col_len, 2 * row_len), bf16)],
        [tiles[0, 0], tile_count, patterns[0, 0]],
        n_smem=2,
        anywhere=(2,),
        scratch=[pltpu.VMEM((slots, words, tile), jnp.int32), pltpu.SemaphoreType.DMA],
        flops=4e9,
    )

    n_far = n_z - 2
    sent, feats_t = call(
        functools.partial(forward_first, n_row, n_z + 2),
        "forward_far_other",
        [((n_far, high, rows), bf16), ((high, col_len), bf16)],
        [st] + feats,
        flops=flops // 4,
    )

    def forward(name, start, count):
        return call(
            functools.partial(forward_more, start), name, [((count, high, rows), bf16)], [st, feats_t], flops=flops // 4
        )[0]

    def pair_sum(name, own, other, count):
        return call(pair_kernel, name, [((high, rows), bf16)] * count, [own, other])

    far = pair_sum("pair_far", forward("forward_far_own", 2, n_far), over_core(sent), n_far)
    far = [over_z(x, k) for k, x in enumerate(far, 2)]
    sent = forward("forward_near_other", n_z, 2)
    near = pair_sum("pair_near", forward("forward_near_own", 0, 2), over_core(sent), 2)
    parts = [near[0], over_z(near[1], 1)] + far

    activated, scaled, grad_agg, agg_t, grad_pre = call(
        functools.partial(dense_kernel, n_z),
        "dense",
        [((rows, width), bf16), ((rows, width), bf16), ((rows, width), f32), ((width, rows), bf16), ((rows, width), bf16)],
        parts + [features, cotangent, weight],
        flops=4 * rows * width * width,
        final=(0,),
    )
    far = [over_z(scaled, k) for k in range(2, n_z)]

    (part,) = call(weight_kernel, "weight_part", [((width, width), bf16)], [agg_t, grad_pre], flops=2e9)
    part = tree_sum([part, over_z(part, 1)]).astype(bf16)
    part = tree_sum([part] + [over_row(part, k) for k in range(1, n_row)]).astype(bf16)
    part = tree_sum([part, over_core(part)]).astype(bf16)

    grads = [scaled, over_z(scaled, 1)]
    grads = grads + [over_core(x) for x in grads]
    (product,) = call(
        functools.partial(backward_near, (0, 1, n_z, n_z + 1)),
        "backward_near",
        [((col_len, width), f32)],
        [st] + grads,
        scratch=[pltpu.VMEM((4 * rows, width), bf16)],
        flops=flops // 2,
    )
    grads = far + [over_core(x) for x in far]
    spots = tuple(range(2, n_z)) + tuple(range(n_z + 2, 2 * n_z))
    backs = call(
        functools.partial(backward_far, spots, n_row),
        "backward_far",
        [((rows, width), bf16)] * n_row,
        [st, product] + grads,
        scratch=[pltpu.VMEM((len(spots) * rows, width), bf16)],
        flops=flops // 2,
    )
    backs, part = lax.optimization_barrier((backs, part))
    for step in range(1, (n_z - 1).bit_length()):
        part = part.astype(bf16)
        part = tree_sum([part, over_z(part, 1 << step)])
    grad_weight = part

    backs = [backs[0]] + [over_row(backs[k], k) for k in range(1, n_row)]
    grad_features = (tree_sum(backs) + grad_agg).astype(bf16)
    return activated, grad_features, grad_weight


def solution(mesh):
    return jax.shard_map(
        per_device,
        mesh=mesh,
        in_specs=(
            P(("row", "col"), None),
            P(),
            P(("row", "col"), None),
            P("row", "col", None, None),
            P("row", "col"),
            P("row", "col", None, None, None),
        ),
        out_specs=(P(("row", "col"), None), P(("row", "col"), None), P()),
        check_vma=False,
    )
```

```python
import functools
import math

import jax
import jax.numpy as jnp
from jax import lax
from jax.experimental import pallas as pl
from jax.experimental.pallas import tpu as pltpu
from jax.sharding import PartitionSpec as P

pad_rows = 16
resident_bytes = 9 << 20
bf16, f32 = jnp.bfloat16, jnp.float32


def fits(shape, dtype):
    return math.prod(shape) * jnp.dtype(dtype).itemsize <= resident_bytes


def smem(count):
    return [pl.BlockSpec(memory_space=pltpu.SMEM)] * count


def call(body, name, outs, args, n_smem=0, anywhere=(), scratch=(), limit=8, flops=1e6, final=()):
    kept = [
        x if i < n_smem or i in anywhere or not fits(x.shape, x.dtype) else pltpu.with_memory_space_constraint(x, pltpu.VMEM)
        for i, x in enumerate(args)
    ]
    shapes = [
        pltpu.VMEM(shape, dtype) if i not in final and fits(shape, dtype) else jax.ShapeDtypeStruct(shape, dtype)
        for i, (shape, dtype) in enumerate(outs)
    ]
    vmem = pl.BlockSpec(memory_space=pltpu.VMEM)
    large = any(not fits(x.shape, x.dtype) for x in args) or any(not fits(*out) for out in outs)
    return pl.pallas_call(
        body,
        out_shape=shapes,
        in_specs=smem(n_smem)
        + [pl.BlockSpec(memory_space=pl.ANY) if i in anywhere else vmem for i in range(n_smem, len(args))],
        out_specs=[vmem] * len(outs),
        scratch_shapes=scratch,
        compiler_params=pltpu.CompilerParams(vmem_limit_bytes=(48 if large else limit) << 20),
        cost_estimate=pl.CostEstimate(flops=int(flops), bytes_accessed=1 << 20, transcendentals=0),
        name=name,
    )(*kept)


def clear(ref):
    rows, width = ref.shape
    step = 128
    zeros = jnp.zeros((step, width), ref.dtype)

    def body(i, _):
        ref[pl.ds(pl.multiple_of(i * step, step), step), :] = zeros
        return 0

    lax.fori_loop(0, rows // step, body, 0)


def unpack_tile(words):
    groups, tile = words.shape
    wide = jnp.broadcast_to(words[:, None, :], (groups, 8, tile))
    shifts = lax.broadcasted_iota(jnp.int32, (groups, 8, tile), 1)
    bits = jnp.bitwise_and(jnp.right_shift(wide, shifts), 1)
    return bits.reshape(groups * 8, tile).astype(jnp.float32).astype(jnp.bfloat16)


def build_kernel(blocks, n_z, tiles, count, patterns, st_ref, held, sem):
    my_row = lax.axis_index("row")
    my_col = lax.axis_index("col")
    my_z, core = my_col // 2, my_col % 2
    tile = patterns.shape[-1]
    copy = pltpu.make_async_copy(patterns, held, sem)
    copy.start()
    clear(st_ref)
    copy.wait()

    def step(t, _):
        a, b = tiles[0, t], tiles[1, t]
        dest = a // blocks
        i0 = ((((dest % 2) ^ core) * n_z + ((dest // 2) ^ my_z)) * blocks + a % blocks) * tile
        k0 = (((b // blocks) ^ my_row) * blocks + b % blocks) * tile
        st_ref[pl.ds(pl.multiple_of(k0, tile), tile), pl.ds(pl.multiple_of(i0, tile), tile)] = unpack_tile(held[t])
        return 0

    lax.fori_loop(0, count[0, 0], step, 0)


def forward_block(feats_t, st_ref, first, rows, width):
    line = lax.broadcasted_iota(jnp.int32, (pad_rows, rows), 0)
    product = jnp.dot(feats_t[...], st_ref[:, first : first + rows], preferred_element_type=f32)
    degree = product[width:]
    high = jnp.floor(degree * (1.0 / 64.0)) * 64.0
    return product[:width].astype(bf16), jnp.where(line == 0, high, jnp.where(line == 1, degree - high, 0.0)).astype(bf16)


def forward_first(n_row, start, *refs):
    st_ref, feats, out, feats_t = refs[0], refs[1 : 1 + n_row], refs[-2], refs[-1]
    rows, width = feats[0].shape
    for i, ref in enumerate(feats):
        feats_t[:width, i * rows : (i + 1) * rows] = ref[...].T
    feats_t[width:, :] = jnp.ones((pad_rows, feats_t.shape[1]), bf16)
    forward_more(start, st_ref, feats_t, out)


def forward_more(start, st_ref, feats_t, out):
    width, rows = out.shape[1] - pad_rows, out.shape[2]
    for j in range(out.shape[0]):
        sums, degree = forward_block(feats_t, st_ref, (start + j) * rows, rows, width)
        out[j, :width, :] = sums
        out[j, width:, :] = degree


def pair_kernel(own, other, *outs):
    for j, out in enumerate(outs):
        out[...] = (own[j].astype(f32) + other[j].astype(f32)).astype(bf16)


def dense_kernel(n_z, *refs):
    parts = refs[:n_z]
    feats, cotangent, weight = refs[n_z : n_z + 3]
    act_ref, scaled_ref, agg_grad_ref, agg_ref, grad_ref = refs[n_z + 3 :]
    width = weight.shape[0]
    total = parts[0][...].astype(f32)
    for part in parts[1:]:
        total = total + part[...].astype(f32)
    degree = total[width : width + 1] + total[width + 1 : width + 2]
    scale = lax.rsqrt(degree + 1.0)
    agg_t = (total[:width] * scale + feats[...].astype(f32).T).astype(bf16)
    agg_ref[...] = agg_t
    w = weight[...]
    preact = jnp.dot(agg_t.T, w, preferred_element_type=f32)
    gate = jax.nn.sigmoid(preact)
    act_ref[...] = (preact * gate).astype(bf16)
    grad_pre = (cotangent[...].astype(f32) * gate * (1.0 + preact * (1.0 - gate))).astype(bf16)
    grad_ref[...] = grad_pre
    grad_agg = lax.dot_general(grad_pre, w, (((1,), (1,)), ((), ())), preferred_element_type=f32)
    agg_grad_ref[...] = grad_agg
    scale_rows = jnp.broadcast_to(scale, agg_t.shape).T
    scaled_ref[...] = (grad_agg * scale_rows).astype(bf16)


def weight_kernel(agg_t, grad_pre, out_ref):
    out_ref[...] = jnp.dot(agg_t[...], grad_pre[...], preferred_element_type=f32).astype(bf16)


def backward_near(spots, *refs):
    st_ref, grads, out = refs[0], refs[1 : 1 + len(spots)], refs[1 + len(spots)]
    gathered = refs[-1]
    rows, _ = grads[0].shape
    for i, ref in enumerate(grads):
        gathered[i * rows : (i + 1) * rows, :] = ref[...]
    for j in range(out.shape[0] // rows):
        lines = slice(j * rows, (j + 1) * rows)
        columns = jnp.concatenate([st_ref[lines, k * rows : (k + 1) * rows] for k in spots], axis=1)
        out[lines, :] = jnp.dot(columns, gathered[...], preferred_element_type=f32)


def backward_far(spots, n_row, *refs):
    st_ref, near, grads, outs = refs[0], refs[1], refs[2 : 2 + len(spots)], refs[2 + len(spots) : 2 + len(spots) + n_row]
    gathered = refs[-1]
    rows, _ = grads[0].shape
    for i, ref in enumerate(grads):
        gathered[i * rows : (i + 1) * rows, :] = ref[...]
    for j, out in enumerate(outs):
        lines = slice(j * rows, (j + 1) * rows)
        columns = jnp.concatenate([st_ref[lines, k * rows : (k + 1) * rows] for k in spots], axis=1)
        out[...] = (near[lines, :] + jnp.dot(columns, gathered[...], preferred_element_type=f32)).astype(out.dtype)


def tree_sum(values):
    values = [x.astype(f32) for x in values]
    while len(values) > 1:
        values = [values[i] + values[i + 1] for i in range(0, len(values), 2)]
    return values[0]


def last_kernel(grad_agg, own, other, *refs):
    total = tree_sum([ref[...] for ref in refs[:-2]])
    refs[-2][...] = (total + grad_agg[...]).astype(bf16)
    refs[-1][...] = own[...].astype(f32) + other[...].astype(f32)


def per_device(features, weight, cotangent, tiles, tile_count, patterns):
    rows, width = features.shape
    slots, words, tile = patterns.shape[2:]
    blocks = rows // tile
    n_row = lax.axis_size("row")
    n_col = lax.axis_size("col")
    n_z = n_col // 2
    row_len = n_z * rows
    col_len = n_row * rows
    flops = 4 * width * col_len * row_len
    high = width + pad_rows

    def over_row(x, k):
        return lax.ppermute(x, "row", [(i, i ^ k) for i in range(n_row)])

    def over_z(x, k):
        return lax.ppermute(x, "col", [(i, i ^ (2 * k)) for i in range(n_col)])

    def over_core(x):
        return lax.ppermute(x, "col", [(i, i ^ 1) for i in range(n_col)])

    feats = [features] + [over_row(features, k) for k in range(1, n_row)]
    (st,) = call(
        functools.partial(build_kernel, blocks, n_z),
        "build",
        [((col_len, 2 * row_len), bf16)],
        [tiles[0, 0], tile_count, patterns[0, 0]],
        n_smem=2,
        anywhere=(2,),
        scratch=[pltpu.VMEM((slots, words, tile), jnp.int32), pltpu.SemaphoreType.DMA],
        flops=4e9,
    )

    n_far = n_z - 2
    sent, feats_t = call(
        functools.partial(forward_first, n_row, n_z + 2),
        "forward_far_other",
        [((n_far, high, rows), bf16), ((high, col_len), bf16)],
        [st] + feats,
        flops=flops // 4,
    )

    def forward(name, start, count):
        return call(
            functools.partial(forward_more, start), name, [((count, high, rows), bf16)], [st, feats_t], flops=flops // 4
        )[0]

    def pair_sum(name, own, other, count):
        return call(pair_kernel, name, [((high, rows), bf16)] * count, [own, other])

    far = pair_sum("pair_far", forward("forward_far_own", 2, n_far), over_core(sent), n_far)
    far = [over_z(x, k) for k, x in enumerate(far, 2)]
    sent = forward("forward_near_other", n_z, 2)
    near = pair_sum("pair_near", forward("forward_near_own", 0, 2), over_core(sent), 2)
    parts = [near[0], over_z(near[1], 1)] + far

    activated, scaled, grad_agg, agg_t, grad_pre = call(
        functools.partial(dense_kernel, n_z),
        "dense",
        [((rows, width), bf16), ((rows, width), bf16), ((rows, width), f32), ((width, rows), bf16), ((rows, width), bf16)],
        parts + [features, cotangent, weight],
        flops=4 * rows * width * width,
    )
    far = [over_z(scaled, k) for k in range(2, n_z)]

    (part,) = call(weight_kernel, "weight_part", [((width, width), bf16)], [agg_t, grad_pre], flops=2e9)
    part = tree_sum([part, over_z(part, 1)]).astype(bf16)
    part = tree_sum([part] + [over_row(part, k) for k in range(1, n_row)]).astype(bf16)
    for step in range(1, (n_z - 1).bit_length()):
        part = tree_sum([part, over_z(part, 1 << step)]).astype(bf16)

    grads = [scaled, over_z(scaled, 1)]
    grads = grads + [over_core(x) for x in grads]
    (product,) = call(
        functools.partial(backward_near, (0, 1, n_z, n_z + 1)),
        "backward_near",
        [((col_len, width), f32)],
        [st] + grads,
        scratch=[pltpu.VMEM((4 * rows, width), bf16)],
        flops=flops // 2,
    )
    grads = far + [over_core(x) for x in far]
    spots = tuple(range(2, n_z)) + tuple(range(n_z + 2, 2 * n_z))
    backs = call(
        functools.partial(backward_far, spots, n_row),
        "backward_far",
        [((rows, width), bf16)] * n_row,
        [st, product] + grads,
        scratch=[pltpu.VMEM((len(spots) * rows, width), bf16)],
        flops=flops // 2,
    )

    backs = [backs[0]] + [over_row(backs[k], k) for k in range(1, n_row)]
    grad_features, grad_weight = call(
        last_kernel,
        "last",
        [((rows, width), bf16), ((width, width), f32)],
        [grad_agg, part, over_core(part)] + backs,
        final=(0, 1),
    )
    return activated, grad_features, grad_weight


def solution(mesh):
    return jax.shard_map(
        per_device,
        mesh=mesh,
        in_specs=(
            P(("row", "col"), None),
            P(),
            P(("row", "col"), None),
            P("row", "col", None, None),
            P("row", "col"),
            P("row", "col", None, None, None),
        ),
        out_specs=(P(("row", "col"), None), P(("row", "col"), None), P()),
        check_vma=False,
    )
```

```python
import functools
import math

import jax
import jax.numpy as jnp
from jax import lax
from jax.experimental import pallas as pl
from jax.experimental.pallas import tpu as pltpu
from jax.sharding import PartitionSpec as P

pad_rows = 16
resident_bytes = 9 << 20
bf16, f32 = jnp.bfloat16, jnp.float32


def fits(shape, dtype):
    return math.prod(shape) * jnp.dtype(dtype).itemsize <= resident_bytes


def smem(count):
    return [pl.BlockSpec(memory_space=pltpu.SMEM)] * count


def call(body, name, outs, args, n_smem=0, anywhere=(), scratch=(), limit=8, flops=1e6, final=()):
    kept = [
        x if i < n_smem or i in anywhere or not fits(x.shape, x.dtype) else pltpu.with_memory_space_constraint(x, pltpu.VMEM)
        for i, x in enumerate(args)
    ]
    shapes = [
        pltpu.VMEM(shape, dtype) if i not in final and fits(shape, dtype) else jax.ShapeDtypeStruct(shape, dtype)
        for i, (shape, dtype) in enumerate(outs)
    ]
    vmem = pl.BlockSpec(memory_space=pltpu.VMEM)
    large = any(not fits(x.shape, x.dtype) for x in args) or any(not fits(*out) for out in outs)
    return pl.pallas_call(
        body,
        out_shape=shapes,
        in_specs=smem(n_smem)
        + [pl.BlockSpec(memory_space=pl.ANY) if i in anywhere else vmem for i in range(n_smem, len(args))],
        out_specs=[vmem] * len(outs),
        scratch_shapes=scratch,
        compiler_params=pltpu.CompilerParams(vmem_limit_bytes=(48 if large else limit) << 20),
        cost_estimate=pl.CostEstimate(flops=int(flops), bytes_accessed=1 << 20, transcendentals=0),
        name=name,
    )(*kept)


def clear(ref):
    rows, width = ref.shape
    step = 128
    zeros = jnp.zeros((step, width), ref.dtype)

    def body(i, _):
        ref[pl.ds(pl.multiple_of(i * step, step), step), :] = zeros
        return 0

    lax.fori_loop(0, rows // step, body, 0)


def unpack_tile(words):
    groups, tile = words.shape
    wide = jnp.broadcast_to(words[:, None, :], (groups, 8, tile))
    shifts = lax.broadcasted_iota(jnp.int32, (groups, 8, tile), 1)
    bits = jnp.bitwise_and(jnp.right_shift(wide, shifts), 1)
    return bits.reshape(groups * 8, tile).astype(jnp.float32).astype(jnp.bfloat16)


def build_kernel(blocks, n_z, tiles, count, patterns, st_ref, held, sem):
    my_row = lax.axis_index("row")
    my_col = lax.axis_index("col")
    my_z, core = my_col // 2, my_col % 2
    tile = patterns.shape[-1]
    copy = pltpu.make_async_copy(patterns, held, sem)
    copy.start()
    clear(st_ref)
    copy.wait()

    def step(t, _):
        a, b = tiles[0, t], tiles[1, t]
        dest = a // blocks
        i0 = ((((dest % 2) ^ core) * n_z + ((dest // 2) ^ my_z)) * blocks + a % blocks) * tile
        k0 = (((b // blocks) ^ my_row) * blocks + b % blocks) * tile
        st_ref[pl.ds(pl.multiple_of(k0, tile), tile), pl.ds(pl.multiple_of(i0, tile), tile)] = unpack_tile(held[t])
        return 0

    lax.fori_loop(0, count[0, 0], step, 0)


def forward_block(feats_t, st_ref, first, rows, width):
    line = lax.broadcasted_iota(jnp.int32, (pad_rows, rows), 0)
    product = jnp.dot(feats_t[...], st_ref[:, first : first + rows], preferred_element_type=f32)
    degree = product[width:]
    high = jnp.floor(degree * (1.0 / 64.0)) * 64.0
    return product[:width].astype(bf16), jnp.where(line == 0, high, jnp.where(line == 1, degree - high, 0.0)).astype(bf16)


def forward_first(n_row, start, *refs):
    st_ref, feats, out, feats_t = refs[0], refs[1 : 1 + n_row], refs[-2], refs[-1]
    rows, width = feats[0].shape
    for i, ref in enumerate(feats):
        feats_t[:width, i * rows : (i + 1) * rows] = ref[...].T
    feats_t[width:, :] = jnp.ones((pad_rows, feats_t.shape[1]), bf16)
    forward_more(start, st_ref, feats_t, out)


def forward_more(start, st_ref, feats_t, out):
    width, rows = out.shape[1] - pad_rows, out.shape[2]
    for j in range(out.shape[0]):
        sums, degree = forward_block(feats_t, st_ref, (start + j) * rows, rows, width)
        out[j, :width, :] = sums
        out[j, width:, :] = degree


def pair_kernel(own, other, *outs):
    for j, out in enumerate(outs):
        out[...] = (own[j].astype(f32) + other[j].astype(f32)).astype(bf16)


def dense_kernel(n_z, *refs):
    parts = refs[:n_z]
    feats, cotangent, weight = refs[n_z : n_z + 3]
    act_ref, scaled_ref, agg_grad_ref, agg_ref, grad_ref = refs[n_z + 3 :]
    width = weight.shape[0]
    total = parts[0][...].astype(f32)
    for part in parts[1:]:
        total = total + part[...].astype(f32)
    degree = total[width : width + 1] + total[width + 1 : width + 2]
    scale = lax.rsqrt(degree + 1.0)
    agg_t = (total[:width] * scale + feats[...].astype(f32).T).astype(bf16)
    agg_ref[...] = agg_t
    w = weight[...]
    preact = jnp.dot(agg_t.T, w, preferred_element_type=f32)
    gate = jax.nn.sigmoid(preact)
    act_ref[...] = (preact * gate).astype(bf16)
    grad_pre = (cotangent[...].astype(f32) * gate * (1.0 + preact * (1.0 - gate))).astype(bf16)
    grad_ref[...] = grad_pre
    grad_agg = lax.dot_general(grad_pre, w, (((1,), (1,)), ((), ())), preferred_element_type=f32)
    agg_grad_ref[...] = grad_agg
    scale_rows = jnp.broadcast_to(scale, agg_t.shape).T
    scaled_ref[...] = (grad_agg * scale_rows).astype(bf16)


def weight_kernel(agg_t, grad_pre, keep_ref, send_ref):
    my_col = lax.axis_index("col")
    core, parity = my_col % 2, (my_col // 2) % 2
    quarter = agg_t.shape[0] // 4
    part = jnp.dot(agg_t[...], grad_pre[...], preferred_element_type=f32).astype(bf16)
    cut = [part[i * quarter : (i + 1) * quarter] for i in range(4)]
    for flip, ref in enumerate((keep_ref, send_ref)):
        here = (core ^ flip) == 0
        first, second = jnp.where(here, cut[0], cut[2]), jnp.where(here, cut[1], cut[3])
        ref[:quarter, :] = jnp.where(parity == 0, first, second)
        ref[quarter:, :] = jnp.where(parity == 0, second, first)


def last_kernel(n_row, grad_agg, *refs):
    backs, quarters, (feat_ref, weight_ref) = refs[:n_row], refs[n_row:-2], refs[-2:]
    feat_ref[...] = (tree_sum([ref[...] for ref in backs]) + grad_agg[...]).astype(bf16)
    my_col = lax.axis_index("col")
    core, parity = my_col % 2, (my_col // 2) % 2
    quarter = quarters[0].shape[0]
    for i, ref in enumerate(quarters):
        at = ((core ^ (i % 2)) * 2 + (parity ^ (i // 2))) * quarter
        weight_ref[pl.ds(pl.multiple_of(at, quarter), quarter), :] = ref[...].astype(f32)


def gather_rows(refs, gathered):
    rows, _ = refs[0].shape
    for i, ref in enumerate(refs):
        gathered[i * rows : (i + 1) * rows, :] = ref[...]


def backward_first(n_z, *refs):
    st_ref, grads, out, gathered = refs[0], refs[1 : 1 + n_z], refs[-2], refs[-1]
    gather_rows(grads, gathered)
    rows = grads[0].shape[0]
    for j in range(out.shape[0] // rows):
        lines = slice(j * rows, (j + 1) * rows)
        out[lines, :] = jnp.dot(st_ref[lines, : n_z * rows], gathered[...], preferred_element_type=f32)


def backward_rest(n_z, n_row, *refs):
    st_ref, product, grads, outs, gathered = refs[0], refs[1], refs[2 : 2 + n_z], refs[2 + n_z : -1], refs[-1]
    gather_rows(grads, gathered)
    rows = grads[0].shape[0]
    for j, out in enumerate(outs):
        lines = slice(j * rows, (j + 1) * rows)
        other = jnp.dot(st_ref[lines, n_z * rows :], gathered[...], preferred_element_type=f32)
        out[...] = (product[lines, :] + other).astype(out.dtype)


def tree_sum(values):
    values = [x.astype(f32) for x in values]
    while len(values) > 1:
        values = [values[i] + values[i + 1] for i in range(0, len(values), 2)]
    return values[0]


def per_device(features, weight, cotangent, tiles, tile_count, patterns):
    rows, width = features.shape
    slots, words, tile = patterns.shape[2:]
    blocks = rows // tile
    n_row = lax.axis_size("row")
    n_col = lax.axis_size("col")
    n_z = n_col // 2
    row_len = n_z * rows
    col_len = n_row * rows
    flops = 4 * width * col_len * row_len
    high = width + pad_rows

    def over_row(x, k):
        return lax.ppermute(x, "row", [(i, i ^ k) for i in range(n_row)])

    def over_z(x, k):
        return lax.ppermute(x, "col", [(i, i ^ (2 * k)) for i in range(n_col)])

    def over_core(x):
        return lax.ppermute(x, "col", [(i, i ^ 1) for i in range(n_col)])

    feats = [features] + [over_row(features, k) for k in range(1, n_row)]
    (st,) = call(
        functools.partial(build_kernel, blocks, n_z),
        "build",
        [((col_len, 2 * row_len), bf16)],
        [tiles[0, 0], tile_count, patterns[0, 0]],
        n_smem=2,
        anywhere=(2,),
        scratch=[pltpu.VMEM((slots, words, tile), jnp.int32), pltpu.SemaphoreType.DMA],
        flops=4e9,
    )

    n_far = n_z - 2
    sent, feats_t = call(
        functools.partial(forward_first, n_row, n_z + 2),
        "forward_far_other",
        [((n_far, high, rows), bf16), ((high, col_len), bf16)],
        [st] + feats,
        flops=flops // 4,
    )

    def forward(name, start, count):
        return call(
            functools.partial(forward_more, start), name, [((count, high, rows), bf16)], [st, feats_t], flops=flops // 4
        )[0]

    def pair_sum(name, own, other, count):
        return call(pair_kernel, name, [((high, rows), bf16)] * count, [own, other])

    far = pair_sum("pair_far", forward("forward_far_own", 2, n_far), over_core(sent), n_far)
    far = [over_z(x, k) for k, x in enumerate(far, 2)]
    sent = forward("forward_near_other", n_z, 2)
    near = pair_sum("pair_near", forward("forward_near_own", 0, 2), over_core(sent), 2)
    parts = [near[0], over_z(near[1], 1)] + far

    activated, scaled, grad_agg, agg_t, grad_pre = call(
        functools.partial(dense_kernel, n_z),
        "dense",
        [((rows, width), bf16), ((rows, width), bf16), ((rows, width), f32), ((width, rows), bf16), ((rows, width), bf16)],
        parts + [features, cotangent, weight],
        flops=4 * rows * width * width,
    )
    far = [over_z(scaled, k) for k in range(2, n_z)]

    keep, send = call(weight_kernel, "weight_part", [((width // 2, width), bf16)] * 2, [agg_t, grad_pre], flops=2e9)
    half = tree_sum([keep, over_core(send)]).astype(bf16)
    quarter = width // 4
    part = tree_sum([half[:quarter], over_z(half[quarter:], 1)]).astype(bf16)
    part = tree_sum([part] + [over_row(part, k) for k in range(1, n_row)]).astype(bf16)
    for step in range(1, (n_z - 1).bit_length()):
        part = tree_sum([part, over_z(part, 1 << step)]).astype(bf16)

    grads = [scaled, over_z(scaled, 1)] + far
    (product,) = call(
        functools.partial(backward_first, n_z),
        "backward_own",
        [((col_len, width), f32)],
        [st] + grads,
        scratch=[pltpu.VMEM((row_len, width), bf16)],
        flops=flops // 2,
    )
    backs = call(
        functools.partial(backward_rest, n_z, n_row),
        "backward_other",
        [((rows, width), bf16)] * n_row,
        [st, product] + [over_core(x) for x in grads],
        scratch=[pltpu.VMEM((row_len, width), bf16)],
        flops=flops // 2,
    )
    backs = [backs[0]] + [over_row(backs[k], k) for k in range(1, n_row)]
    straight = lax.ppermute(part, "col", [(i, i ^ 3) for i in range(n_col)])
    grad_features, grad_weight = call(
        functools.partial(last_kernel, n_row),
        "last",
        [((rows, width), bf16), ((width, width), f32)],
        [grad_agg] + backs + [part, over_core(part), over_z(part, 1), straight],
        final=(0, 1),
    )
    return activated, grad_features, grad_weight


def solution(mesh):
    return jax.shard_map(
        per_device,
        mesh=mesh,
        in_specs=(
            P(("row", "col"), None),
            P(),
            P(("row", "col"), None),
            P("row", "col", None, None),
            P("row", "col"),
            P("row", "col", None, None, None),
        ),
        out_specs=(P(("row", "col"), None), P(("row", "col"), None), P()),
        check_vma=False,
    )
```

```python
import functools
import math

import jax
import jax.numpy as jnp
from jax import lax
from jax.experimental import pallas as pl
from jax.experimental.pallas import tpu as pltpu
from jax.sharding import PartitionSpec as P

pad_rows = 16
resident_bytes = 9 << 20
bf16, f32 = jnp.bfloat16, jnp.float32


def fits(shape, dtype):
    return math.prod(shape) * jnp.dtype(dtype).itemsize <= resident_bytes


def smem(count):
    return [pl.BlockSpec(memory_space=pltpu.SMEM)] * count


def call(body, name, outs, args, n_smem=0, anywhere=(), scratch=(), limit=8, flops=1e6, final=()):
    kept = [
        x if i < n_smem or i in anywhere or not fits(x.shape, x.dtype) else pltpu.with_memory_space_constraint(x, pltpu.VMEM)
        for i, x in enumerate(args)
    ]
    shapes = [
        pltpu.VMEM(shape, dtype) if i not in final and fits(shape, dtype) else jax.ShapeDtypeStruct(shape, dtype)
        for i, (shape, dtype) in enumerate(outs)
    ]
    vmem = pl.BlockSpec(memory_space=pltpu.VMEM)
    large = any(not fits(x.shape, x.dtype) for x in args) or any(not fits(*out) for out in outs)
    return pl.pallas_call(
        body,
        out_shape=shapes,
        in_specs=smem(n_smem)
        + [pl.BlockSpec(memory_space=pl.ANY) if i in anywhere else vmem for i in range(n_smem, len(args))],
        out_specs=[vmem] * len(outs),
        scratch_shapes=scratch,
        compiler_params=pltpu.CompilerParams(vmem_limit_bytes=(48 if large else limit) << 20),
        cost_estimate=pl.CostEstimate(flops=int(flops), bytes_accessed=1 << 20, transcendentals=0),
        name=name,
    )(*kept)


def clear(ref):
    rows, width = ref.shape
    step = 128
    zeros = jnp.zeros((step, width), ref.dtype)

    def body(i, _):
        ref[pl.ds(pl.multiple_of(i * step, step), step), :] = zeros
        return 0

    lax.fori_loop(0, rows // step, body, 0)


def unpack_tile(words):
    groups, tile = words.shape
    wide = jnp.broadcast_to(words[:, None, :], (groups, 8, tile))
    shifts = lax.broadcasted_iota(jnp.int32, (groups, 8, tile), 1)
    bits = jnp.bitwise_and(jnp.right_shift(wide, shifts), 1)
    return bits.reshape(groups * 8, tile).astype(jnp.float32).astype(jnp.bfloat16)


def build_kernel(blocks, n_z, tiles, count, patterns, st_ref, held, sem):
    my_row = lax.axis_index("row")
    my_col = lax.axis_index("col")
    my_z, core = my_col // 2, my_col % 2
    tile = patterns.shape[-1]
    copy = pltpu.make_async_copy(patterns, held, sem)
    copy.start()
    clear(st_ref)
    copy.wait()

    def step(t, _):
        a, b = tiles[0, t], tiles[1, t]
        dest = a // blocks
        i0 = ((((dest % 2) ^ core) * n_z + ((dest // 2) ^ my_z)) * blocks + a % blocks) * tile
        k0 = (((b // blocks) ^ my_row) * blocks + b % blocks) * tile
        st_ref[pl.ds(pl.multiple_of(k0, tile), tile), pl.ds(pl.multiple_of(i0, tile), tile)] = unpack_tile(held[t])
        return 0

    lax.fori_loop(0, count[0, 0], step, 0)


def forward_block(feats_t, st_ref, first, rows, width):
    line = lax.broadcasted_iota(jnp.int32, (pad_rows, rows), 0)
    product = jnp.dot(feats_t[...], st_ref[:, first : first + rows], preferred_element_type=f32)
    degree = product[width:]
    high = jnp.floor(degree * (1.0 / 64.0)) * 64.0
    return product[:width].astype(bf16), jnp.where(line == 0, high, jnp.where(line == 1, degree - high, 0.0)).astype(bf16)


def forward_first(n_row, start, *refs):
    st_ref, feats, out, feats_t = refs[0], refs[1 : 1 + n_row], refs[-2], refs[-1]
    rows, width = feats[0].shape
    for i, ref in enumerate(feats):
        feats_t[:width, i * rows : (i + 1) * rows] = ref[...].T
    feats_t[width:, :] = jnp.ones((pad_rows, feats_t.shape[1]), bf16)
    forward_more(start, st_ref, feats_t, out)


def forward_more(start, st_ref, feats_t, out):
    width, rows = out.shape[1] - pad_rows, out.shape[2]
    for j in range(out.shape[0]):
        sums, degree = forward_block(feats_t, st_ref, (start + j) * rows, rows, width)
        out[j, :width, :] = sums
        out[j, width:, :] = degree


def pair_kernel(own, other, *outs):
    for j, out in enumerate(outs):
        out[...] = (own[j].astype(f32) + other[j].astype(f32)).astype(bf16)


def dense_kernel(n_z, *refs):
    parts = refs[:n_z]
    feats, cotangent, weight = refs[n_z : n_z + 3]
    act_ref, scaled_ref, agg_grad_ref, agg_ref, grad_ref = refs[n_z + 3 :]
    width = weight.shape[0]
    total = parts[0][...].astype(f32)
    for part in parts[1:]:
        total = total + part[...].astype(f32)
    degree = total[width : width + 1] + total[width + 1 : width + 2]
    scale = lax.rsqrt(degree + 1.0)
    agg_t = (total[:width] * scale + feats[...].astype(f32).T).astype(bf16)
    agg_ref[...] = agg_t
    w = weight[...]
    preact = jnp.dot(agg_t.T, w, preferred_element_type=f32)
    gate = jax.nn.sigmoid(preact)
    act_ref[...] = (preact * gate).astype(bf16)
    grad_pre = (cotangent[...].astype(f32) * gate * (1.0 + preact * (1.0 - gate))).astype(bf16)
    grad_ref[...] = grad_pre
    grad_agg = lax.dot_general(grad_pre, w, (((1,), (1,)), ((), ())), preferred_element_type=f32)
    agg_grad_ref[...] = grad_agg
    scale_rows = jnp.broadcast_to(scale, agg_t.shape).T
    scaled_ref[...] = (grad_agg * scale_rows).astype(bf16)


def weight_kernel(agg_t, grad_pre, keep_ref, send_ref):
    my_col = lax.axis_index("col")
    core, parity = my_col % 2, (my_col // 2) % 2
    quarter = agg_t.shape[0] // 4
    part = jnp.dot(agg_t[...], grad_pre[...], preferred_element_type=f32).astype(bf16)
    cut = [part[i * quarter : (i + 1) * quarter] for i in range(4)]
    for flip, ref in enumerate((keep_ref, send_ref)):
        here = (core ^ flip) == 0
        first, second = jnp.where(here, cut[0], cut[2]), jnp.where(here, cut[1], cut[3])
        ref[:quarter, :] = jnp.where(parity == 0, first, second)
        ref[quarter:, :] = jnp.where(parity == 0, second, first)


def last_kernel(n_row, grad_agg, *refs):
    backs, quarters, (feat_ref, weight_ref) = refs[:n_row], refs[n_row:-2], refs[-2:]
    feat_ref[...] = (tree_sum([ref[...] for ref in backs]) + grad_agg[...]).astype(bf16)
    my_col = lax.axis_index("col")
    core, parity = my_col % 2, (my_col // 2) % 2
    quarter = quarters[0].shape[0]
    for i, ref in zip((0, 1, 2, 3), quarters):
        at = ((core ^ (i % 2)) * 2 + (parity ^ (i // 2))) * quarter
        weight_ref[pl.ds(pl.multiple_of(at, quarter), quarter), :] = ref[...].astype(f32)


def gather_rows(refs, gathered, order):
    rows, _ = refs[0].shape
    for i, ref in zip(order, refs):
        gathered[i * rows : (i + 1) * rows, :] = ref[...]


def backward_first(n_z, order, *refs):
    st_ref, grads, out, gathered = refs[0], refs[1 : 1 + n_z], refs[-2], refs[-1]
    gather_rows(grads, gathered, order)
    rows = grads[0].shape[0]
    for j in range(out.shape[0] // rows):
        lines = slice(j * rows, (j + 1) * rows)
        out[lines, :] = jnp.dot(st_ref[lines, : n_z * rows], gathered[...], preferred_element_type=f32)


def backward_rest(n_z, n_row, order, *refs):
    st_ref, product, grads, outs, gathered = refs[0], refs[1], refs[2 : 2 + n_z], refs[2 + n_z : -1], refs[-1]
    gather_rows(grads, gathered, order)
    rows = grads[0].shape[0]
    for j, out in enumerate(outs):
        lines = slice(j * rows, (j + 1) * rows)
        other = jnp.dot(st_ref[lines, n_z * rows :], gathered[...], preferred_element_type=f32)
        out[...] = (product[lines, :] + other).astype(out.dtype)


def tree_sum(values):
    values = [x.astype(f32) for x in values]
    while len(values) > 1:
        values = [values[i] + values[i + 1] for i in range(0, len(values), 2)]
    return values[0]


def per_device(features, weight, cotangent, tiles, tile_count, patterns):
    rows, width = features.shape
    slots, words, tile = patterns.shape[2:]
    blocks = rows // tile
    n_row = lax.axis_size("row")
    n_col = lax.axis_size("col")
    n_z = n_col // 2
    row_len = n_z * rows
    col_len = n_row * rows
    flops = 4 * width * col_len * row_len
    high = width + pad_rows

    def over_row(x, k):
        return lax.ppermute(x, "row", [(i, i ^ k) for i in range(n_row)])

    def over_z(x, k):
        return lax.ppermute(x, "col", [(i, i ^ (2 * k)) for i in range(n_col)])

    def over_core(x):
        return lax.ppermute(x, "col", [(i, i ^ 1) for i in range(n_col)])

    feats = [features] + [over_row(features, k) for k in range(1, n_row)]
    (st,) = call(
        functools.partial(build_kernel, blocks, n_z),
        "build",
        [((col_len, 2 * row_len), bf16)],
        [tiles[0, 0], tile_count, patterns[0, 0]],
        n_smem=2,
        anywhere=(2,),
        scratch=[pltpu.VMEM((slots, words, tile), jnp.int32), pltpu.SemaphoreType.DMA],
        flops=4e9,
    )

    n_far = n_z - 2
    sent, feats_t = call(
        functools.partial(forward_first, n_row, n_z + 2),
        "forward_far_other",
        [((n_far, high, rows), bf16), ((high, col_len), bf16)],
        [st] + feats,
        flops=flops // 4,
    )

    def forward(name, start, count):
        return call(
            functools.partial(forward_more, start), name, [((count, high, rows), bf16)], [st, feats_t], flops=flops // 4
        )[0]

    def pair_sum(name, own, other, count):
        return call(pair_kernel, name, [((high, rows), bf16)] * count, [own, other])

    far = pair_sum("pair_far", forward("forward_far_own", 2, n_far), over_core(sent), n_far)
    far = [over_z(x, k) for k, x in enumerate(far, 2)]
    sent = forward("forward_near_other", n_z, 2)
    near = pair_sum("pair_near", forward("forward_near_own", 0, 2), over_core(sent), 2)
    parts = [near[0], over_z(near[1], 1)] + far

    activated, scaled, grad_agg, agg_t, grad_pre = call(
        functools.partial(dense_kernel, n_z),
        "dense",
        [((rows, width), bf16), ((rows, width), bf16), ((rows, width), f32), ((width, rows), bf16), ((rows, width), bf16)],
        parts + [features, cotangent, weight],
        flops=4 * rows * width * width,
    )
    far = [over_z(scaled, k) for k in range(2, n_z)]

    keep, send = call(weight_kernel, "weight_part", [((width // 2, width), bf16)] * 2, [agg_t, grad_pre], flops=2e9)
    half = tree_sum([keep, over_core(send)]).astype(bf16)
    quarter = width // 4
    part = tree_sum([half[:quarter], over_z(half[quarter:], 1)]).astype(bf16)
    part = tree_sum([part] + [over_row(part, k) for k in reversed(range(1, n_row))][::-1]).astype(bf16)
    row_sum = part

    order_own = [0, 1, 2, 3] + list(range(4, n_z))
    order_other = [2, 3, 1, 0] + list(range(4, n_z))
    grads = [scaled, over_z(scaled, 1)] + far
    (product,) = call(
        functools.partial(backward_first, n_z, order_own),
        "backward_own",
        [((col_len, width), f32)],
        [st] + [grads[z] for z in order_own],
        scratch=[pltpu.VMEM((row_len, width), bf16)],
        flops=flops // 2,
    )
    product, part = lax.optimization_barrier((product, row_sum))
    for step in range(1, (n_z - 1).bit_length()):
        part = tree_sum([part, over_z(part, 1 << step)]).astype(bf16)
    backs = call(
        functools.partial(backward_rest, n_z, n_row, order_other),
        "backward_other",
        [((rows, width), bf16)] * n_row,
        [st, product] + [over_core(grads[z]) for z in order_other],
        scratch=[pltpu.VMEM((row_len, width), bf16)],
        flops=flops // 2,
    )
    backs = [backs[0]] + [over_row(backs[k], k) for k in range(1, n_row)]
    straight = lax.ppermute(part, "col", [(i, i ^ 3) for i in range(n_col)])
    grad_features, grad_weight = call(
        functools.partial(last_kernel, n_row),
        "last",
        [((rows, width), bf16), ((width, width), f32)],
        [grad_agg] + backs + [part, over_core(part), over_z(part, 1), straight],
        final=(0, 1),
    )
    return activated, grad_features, grad_weight


def solution(mesh):
    return jax.shard_map(
        per_device,
        mesh=mesh,
        in_specs=(
            P(("row", "col"), None),
            P(),
            P(("row", "col"), None),
            P("row", "col", None, None),
            P("row", "col"),
            P("row", "col", None, None, None),
        ),
        out_specs=(P(("row", "col"), None), P(("row", "col"), None), P()),
        check_vma=False,
    )
```

```python
import functools
import math

import jax
import jax.numpy as jnp
from jax import lax
from jax.experimental import pallas as pl
from jax.experimental.pallas import tpu as pltpu
from jax.sharding import PartitionSpec as P

pad_rows = 16
resident_bytes = 9 << 20
bf16, f32 = jnp.bfloat16, jnp.float32


def fits(shape, dtype):
    return math.prod(shape) * jnp.dtype(dtype).itemsize <= resident_bytes


def smem(count):
    return [pl.BlockSpec(memory_space=pltpu.SMEM)] * count


def call(body, name, outs, args, n_smem=0, anywhere=(), scratch=(), limit=8, flops=1e6, final=()):
    kept = [
        x if i < n_smem or i in anywhere or not fits(x.shape, x.dtype) else pltpu.with_memory_space_constraint(x, pltpu.VMEM)
        for i, x in enumerate(args)
    ]
    shapes = [
        pltpu.VMEM(shape, dtype) if i not in final and fits(shape, dtype) else jax.ShapeDtypeStruct(shape, dtype)
        for i, (shape, dtype) in enumerate(outs)
    ]
    vmem = pl.BlockSpec(memory_space=pltpu.VMEM)
    large = any(not fits(x.shape, x.dtype) for x in args) or any(not fits(*out) for out in outs)
    return pl.pallas_call(
        body,
        out_shape=shapes,
        in_specs=smem(n_smem)
        + [pl.BlockSpec(memory_space=pl.ANY) if i in anywhere else vmem for i in range(n_smem, len(args))],
        out_specs=[vmem] * len(outs),
        scratch_shapes=scratch,
        compiler_params=pltpu.CompilerParams(vmem_limit_bytes=(48 if large else limit) << 20),
        cost_estimate=pl.CostEstimate(flops=int(flops), bytes_accessed=1 << 20, transcendentals=0),
        name=name,
    )(*kept)


def clear(ref):
    rows, width = ref.shape
    step = 128
    zeros = jnp.zeros((step, width), ref.dtype)

    def body(i, _):
        ref[pl.ds(pl.multiple_of(i * step, step), step), :] = zeros
        return 0

    lax.fori_loop(0, rows // step, body, 0)


def unpack_tile(words):
    groups, tile = words.shape
    wide = jnp.broadcast_to(words[:, None, :], (groups, 8, tile))
    shifts = lax.broadcasted_iota(jnp.int32, (groups, 8, tile), 1)
    bits = jnp.bitwise_and(jnp.right_shift(wide, shifts), 1)
    return bits.reshape(groups * 8, tile).astype(jnp.float32).astype(jnp.bfloat16)


def build_kernel(blocks, n_z, tiles, count, patterns, st_ref, held, sem):
    my_row = lax.axis_index("row")
    my_col = lax.axis_index("col")
    my_z, core = my_col // 2, my_col % 2
    tile = patterns.shape[-1]
    copy = pltpu.make_async_copy(patterns, held, sem)
    copy.start()
    clear(st_ref)
    copy.wait()

    def step(t, _):
        a, b = tiles[0, t], tiles[1, t]
        dest = a // blocks
        i0 = ((((dest % 2) ^ core) * n_z + ((dest // 2) ^ my_z)) * blocks + a % blocks) * tile
        k0 = (((b // blocks) ^ my_row) * blocks + b % blocks) * tile
        st_ref[pl.ds(pl.multiple_of(k0, tile), tile), pl.ds(pl.multiple_of(i0, tile), tile)] = unpack_tile(held[t])
        return 0

    lax.fori_loop(0, count[0, 0], step, 0)


def forward_block(feats_t, st_ref, first, rows, width):
    line = lax.broadcasted_iota(jnp.int32, (pad_rows, rows), 0)
    product = jnp.dot(feats_t[...], st_ref[:, first : first + rows], preferred_element_type=f32)
    degree = product[width:]
    high = jnp.floor(degree * (1.0 / 64.0)) * 64.0
    return product[:width].astype(bf16), jnp.where(line == 0, high, jnp.where(line == 1, degree - high, 0.0)).astype(bf16)


def forward_first(n_row, start, *refs):
    st_ref, feats, out, feats_t = refs[0], refs[1 : 1 + n_row], refs[-2], refs[-1]
    rows, width = feats[0].shape
    for i, ref in enumerate(feats):
        feats_t[:width, i * rows : (i + 1) * rows] = ref[...].T
    feats_t[width:, :] = jnp.ones((pad_rows, feats_t.shape[1]), bf16)
    forward_more(start, st_ref, feats_t, out)


def forward_more(start, st_ref, feats_t, out):
    width, rows = out.shape[1] - pad_rows, out.shape[2]
    for j in range(out.shape[0]):
        sums, degree = forward_block(feats_t, st_ref, (start + j) * rows, rows, width)
        out[j, :width, :] = sums
        out[j, width:, :] = degree


def pair_kernel(own, other, *outs):
    for j, out in enumerate(outs):
        out[...] = (own[j].astype(f32) + other[j].astype(f32)).astype(bf16)


def dense_kernel(n_z, *refs):
    parts = refs[:n_z]
    feats, cotangent, weight = refs[n_z : n_z + 3]
    act_ref, scaled_ref, agg_grad_ref, keep_ref, send_ref = refs[n_z + 3 :]
    width = weight.shape[0]
    total = parts[0][...].astype(f32)
    for part in parts[1:]:
        total = total + part[...].astype(f32)
    degree = total[width : width + 1] + total[width + 1 : width + 2]
    scale = lax.rsqrt(degree + 1.0)
    agg_t = (total[:width] * scale + feats[...].astype(f32).T).astype(bf16)
    w = weight[...]
    preact = jnp.dot(agg_t.T, w, preferred_element_type=f32)
    gate = jax.nn.sigmoid(preact)
    act_ref[...] = (preact * gate).astype(bf16)
    grad_pre = (cotangent[...].astype(f32) * gate * (1.0 + preact * (1.0 - gate))).astype(bf16)
    grad_agg = lax.dot_general(grad_pre, w, (((1,), (1,)), ((), ())), preferred_element_type=f32)
    agg_grad_ref[...] = grad_agg
    scale_rows = jnp.broadcast_to(scale, agg_t.shape).T
    scaled_ref[...] = (grad_agg * scale_rows).astype(bf16)
    weight_quarters(agg_t, grad_pre, keep_ref, send_ref)


def weight_quarters(agg_t, grad_pre, keep_ref, send_ref):
    my_col = lax.axis_index("col")
    core, parity = my_col % 2, (my_col // 2) % 2
    quarter = agg_t.shape[0] // 4
    part = jnp.dot(agg_t, grad_pre, preferred_element_type=f32).astype(bf16)
    cut = [part[i * quarter : (i + 1) * quarter] for i in range(4)]
    for flip, ref in enumerate((keep_ref, send_ref)):
        here = (core ^ flip) == 0
        first, second = jnp.where(here, cut[0], cut[2]), jnp.where(here, cut[1], cut[3])
        ref[:quarter, :] = jnp.where(parity == 0, first, second)
        ref[quarter:, :] = jnp.where(parity == 0, second, first)


def last_kernel(n_row, grad_agg, *refs):
    backs, quarters, (feat_ref, weight_ref) = refs[:n_row], refs[n_row:-2], refs[-2:]
    feat_ref[...] = (tree_sum([ref[...] for ref in backs]) + grad_agg[...]).astype(bf16)
    my_col = lax.axis_index("col")
    core, parity = my_col % 2, (my_col // 2) % 2
    quarter = quarters[0].shape[0]
    for i, ref in zip((0, 1, 2, 3), quarters):
        at = ((core ^ (i % 2)) * 2 + (parity ^ (i // 2))) * quarter
        weight_ref[pl.ds(pl.multiple_of(at, quarter), quarter), :] = ref[...].astype(f32)


def gather_rows(refs, gathered, order):
    rows, _ = refs[0].shape
    for i, ref in zip(order, refs):
        gathered[i * rows : (i + 1) * rows, :] = ref[...]


def backward_first(n_z, order, *refs):
    st_ref, grads, out, gathered = refs[0], refs[1 : 1 + n_z], refs[-2], refs[-1]
    gather_rows(grads, gathered, order)
    rows = grads[0].shape[0]
    for j in range(out.shape[0] // rows):
        lines = slice(j * rows, (j + 1) * rows)
        out[lines, :] = jnp.dot(st_ref[lines, : n_z * rows], gathered[...], preferred_element_type=f32)


def backward_rest(n_z, n_row, order, *refs):
    st_ref, product, grads, outs, gathered = refs[0], refs[1], refs[2 : 2 + n_z], refs[2 + n_z : -1], refs[-1]
    gather_rows(grads, gathered, order)
    rows = grads[0].shape[0]
    for j, out in enumerate(outs):
        lines = slice(j * rows, (j + 1) * rows)
        other = jnp.dot(st_ref[lines, n_z * rows :], gathered[...], preferred_element_type=f32)
        out[...] = (product[lines, :] + other).astype(out.dtype)


def tree_sum(values):
    values = [x.astype(f32) for x in values]
    while len(values) > 1:
        values = [values[i] + values[i + 1] for i in range(0, len(values), 2)]
    return values[0]


def per_device(features, weight, cotangent, tiles, tile_count, patterns):
    rows, width = features.shape
    slots, words, tile = patterns.shape[2:]
    blocks = rows // tile
    n_row = lax.axis_size("row")
    n_col = lax.axis_size("col")
    n_z = n_col // 2
    row_len = n_z * rows
    col_len = n_row * rows
    flops = 4 * width * col_len * row_len
    high = width + pad_rows

    def over_row(x, k):
        return lax.ppermute(x, "row", [(i, i ^ k) for i in range(n_row)])

    def over_z(x, k):
        return lax.ppermute(x, "col", [(i, i ^ (2 * k)) for i in range(n_col)])

    def over_core(x):
        return lax.ppermute(x, "col", [(i, i ^ 1) for i in range(n_col)])

    feats = [features] + [over_row(features, k) for k in range(1, n_row)]
    (st,) = call(
        functools.partial(build_kernel, blocks, n_z),
        "build",
        [((col_len, 2 * row_len), bf16)],
        [tiles[0, 0], tile_count, patterns[0, 0]],
        n_smem=2,
        anywhere=(2,),
        scratch=[pltpu.VMEM((slots, words, tile), jnp.int32), pltpu.SemaphoreType.DMA],
        flops=4e9,
    )

    n_far = n_z - 2
    sent, feats_t = call(
        functools.partial(forward_first, n_row, n_z + 2),
        "forward_far_other",
        [((n_far, high, rows), bf16), ((high, col_len), bf16)],
        [st] + feats,
        flops=flops // 4,
    )

    def forward(name, start, count):
        return call(
            functools.partial(forward_more, start), name, [((count, high, rows), bf16)], [st, feats_t], flops=flops // 4
        )[0]

    def pair_sum(name, own, other, count):
        return call(pair_kernel, name, [((high, rows), bf16)] * count, [own, other])

    far = pair_sum("pair_far", forward("forward_far_own", 2, n_far), over_core(sent), n_far)
    far = [over_z(x, k) for k, x in enumerate(far, 2)]
    sent = forward("forward_near_other", n_z, 2)
    near = pair_sum("pair_near", forward("forward_near_own", 0, 2), over_core(sent), 2)
    parts = [near[0], over_z(near[1], 1)] + far

    activated, scaled, grad_agg, keep, send = call(
        functools.partial(dense_kernel, n_z),
        "dense",
        [((rows, width), bf16), ((rows, width), bf16), ((rows, width), f32)] + [((width // 2, width), bf16)] * 2,
        parts + [features, cotangent, weight],
        flops=4 * rows * width * width,
    )
    far = [over_z(scaled, k) for k in range(2, n_z)]

    half = tree_sum([keep, over_core(send)]).astype(bf16)
    quarter = width // 4
    part = tree_sum([half[:quarter], over_z(half[quarter:], 1)]).astype(bf16)
    part = tree_sum([part] + [over_row(part, k) for k in reversed(range(1, n_row))][::-1]).astype(bf16)
    row_sum = part

    order_own = [0, 1, 2, 3] + list(range(4, n_z))
    order_other = [2, 3, 1, 0] + list(range(4, n_z))
    grads = [scaled, over_z(scaled, 1)] + far
    (product,) = call(
        functools.partial(backward_first, n_z, order_own),
        "backward_own",
        [((col_len, width), f32)],
        [st] + [grads[z] for z in order_own],
        scratch=[pltpu.VMEM((row_len, width), bf16)],
        flops=flops // 2,
    )
    product, part = lax.optimization_barrier((product, row_sum))
    for step in range(1, (n_z - 1).bit_length()):
        part = tree_sum([part, over_z(part, 1 << step)]).astype(bf16)
    backs = call(
        functools.partial(backward_rest, n_z, n_row, order_other),
        "backward_other",
        [((rows, width), bf16)] * n_row,
        [st, product] + [over_core(grads[z]) for z in order_other],
        scratch=[pltpu.VMEM((row_len, width), bf16)],
        flops=flops // 2,
    )
    backs = [backs[0]] + [over_row(backs[k], k) for k in range(1, n_row)]
    straight = lax.ppermute(part, "col", [(i, i ^ 3) for i in range(n_col)])
    grad_features, grad_weight = call(
        functools.partial(last_kernel, n_row),
        "last",
        [((rows, width), bf16), ((width, width), f32)],
        [grad_agg] + backs + [part, over_core(part), over_z(part, 1), straight],
        final=(0, 1),
    )
    return activated, grad_features, grad_weight


def solution(mesh):
    return jax.shard_map(
        per_device,
        mesh=mesh,
        in_specs=(
            P(("row", "col"), None),
            P(),
            P(("row", "col"), None),
            P("row", "col", None, None),
            P("row", "col"),
            P("row", "col", None, None, None),
        ),
        out_specs=(P(("row", "col"), None), P(("row", "col"), None), P()),
        check_vma=False,
    )
```

```python
import functools
import math

import jax
import jax.numpy as jnp
from jax import lax
from jax.experimental import pallas as pl
from jax.experimental.pallas import tpu as pltpu
from jax.sharding import PartitionSpec as P

pad_rows = 16
resident_bytes = 9 << 20
bf16, f32 = jnp.bfloat16, jnp.float32


def fits(shape, dtype):
    return math.prod(shape) * jnp.dtype(dtype).itemsize <= resident_bytes


def smem(count):
    return [pl.BlockSpec(memory_space=pltpu.SMEM)] * count


def call(body, name, outs, args, n_smem=0, anywhere=(), scratch=(), limit=8, flops=1e6, final=()):
    kept = [
        x if i < n_smem or i in anywhere or not fits(x.shape, x.dtype) else pltpu.with_memory_space_constraint(x, pltpu.VMEM)
        for i, x in enumerate(args)
    ]
    shapes = [
        pltpu.VMEM(shape, dtype) if i not in final and fits(shape, dtype) else jax.ShapeDtypeStruct(shape, dtype)
        for i, (shape, dtype) in enumerate(outs)
    ]
    vmem = pl.BlockSpec(memory_space=pltpu.VMEM)
    large = any(not fits(x.shape, x.dtype) for x in args) or any(not fits(*out) for out in outs)
    return pl.pallas_call(
        body,
        out_shape=shapes,
        in_specs=smem(n_smem)
        + [pl.BlockSpec(memory_space=pl.ANY) if i in anywhere else vmem for i in range(n_smem, len(args))],
        out_specs=[vmem] * len(outs),
        scratch_shapes=scratch,
        compiler_params=pltpu.CompilerParams(vmem_limit_bytes=(48 if large else limit) << 20),
        cost_estimate=pl.CostEstimate(flops=int(flops), bytes_accessed=1 << 20, transcendentals=0),
        name=name,
    )(*kept)


def clear(ref):
    rows, width = ref.shape
    step = 128
    zeros = jnp.zeros((step, width), ref.dtype)

    def body(i, _):
        ref[pl.ds(pl.multiple_of(i * step, step), step), :] = zeros
        return 0

    lax.fori_loop(0, rows // step, body, 0)


def unpack_tile(words):
    groups, tile = words.shape
    wide = jnp.broadcast_to(words[:, None, :], (groups, 8, tile))
    shifts = lax.broadcasted_iota(jnp.int32, (groups, 8, tile), 1)
    bits = jnp.bitwise_and(jnp.right_shift(wide, shifts), 1)
    return bits.reshape(groups * 8, tile).astype(jnp.float32).astype(jnp.bfloat16)


def build_kernel(blocks, n_z, tiles, count, patterns, st_ref, held, sem):
    my_row = lax.axis_index("row")
    my_col = lax.axis_index("col")
    my_z, core = my_col // 2, my_col % 2
    tile = patterns.shape[-1]
    copy = pltpu.make_async_copy(patterns, held, sem)
    copy.start()
    clear(st_ref)
    copy.wait()

    def step(t, _):
        a, b = tiles[0, t], tiles[1, t]
        dest = a // blocks
        i0 = ((((dest % 2) ^ core) * n_z + ((dest // 2) ^ my_z)) * blocks + a % blocks) * tile
        k0 = (((b // blocks) ^ my_row) * blocks + b % blocks) * tile
        st_ref[pl.ds(pl.multiple_of(k0, tile), tile), pl.ds(pl.multiple_of(i0, tile), tile)] = unpack_tile(held[t])
        return 0

    lax.fori_loop(0, count[0, 0], step, 0)


def forward_block(feats_t, st_ref, first, rows, width):
    line = lax.broadcasted_iota(jnp.int32, (pad_rows, rows), 0)
    product = jnp.dot(feats_t[...], st_ref[:, first : first + rows], preferred_element_type=f32)
    degree = product[width:]
    high = jnp.floor(degree * (1.0 / 64.0)) * 64.0
    return product[:width].astype(bf16), jnp.where(line == 0, high, jnp.where(line == 1, degree - high, 0.0)).astype(bf16)


def forward_first(n_row, start, *refs):
    st_ref, feats, out, feats_t = refs[0], refs[1 : 1 + n_row], refs[-2], refs[-1]
    rows, width = feats[0].shape
    for i, ref in enumerate(feats):
        feats_t[:width, i * rows : (i + 1) * rows] = ref[...].T
    feats_t[width:, :] = jnp.ones((pad_rows, feats_t.shape[1]), bf16)
    forward_more(start, st_ref, feats_t, out)


def forward_more(start, st_ref, feats_t, out):
    width, rows = out.shape[1] - pad_rows, out.shape[2]
    for j in range(out.shape[0]):
        sums, degree = forward_block(feats_t, st_ref, (start + j) * rows, rows, width)
        out[j, :width, :] = sums
        out[j, width:, :] = degree


def pair_kernel(own, other, *outs):
    for j, out in enumerate(outs):
        out[...] = (own[j].astype(f32) + other[j].astype(f32)).astype(bf16)


def dense_kernel(n_z, *refs):
    parts = refs[:n_z]
    feats, cotangent, weight = refs[n_z : n_z + 3]
    act_ref, scaled_ref, agg_grad_ref, agg_ref, grad_ref = refs[n_z + 3 :]
    width = weight.shape[0]
    total = parts[0][...].astype(f32)
    for part in parts[1:]:
        total = total + part[...].astype(f32)
    degree = total[width : width + 1] + total[width + 1 : width + 2]
    scale = lax.rsqrt(degree + 1.0)
    agg_t = (total[:width] * scale + feats[:width, : cotangent.shape[0]].astype(f32)).astype(bf16)
    agg_ref[...] = agg_t
    w = weight[...]
    preact = jnp.dot(agg_t.T, w, preferred_element_type=f32)
    gate = jax.nn.sigmoid(preact)
    act_ref[...] = (preact * gate).astype(bf16)
    grad_pre = (cotangent[...].astype(f32) * gate * (1.0 + preact * (1.0 - gate))).astype(bf16)
    grad_ref[...] = grad_pre
    grad_agg = lax.dot_general(grad_pre, w, (((1,), (1,)), ((), ())), preferred_element_type=f32)
    agg_grad_ref[...] = grad_agg
    scale_rows = jnp.broadcast_to(scale, agg_t.shape).T
    scaled_ref[...] = (grad_agg * scale_rows).astype(bf16)


def weight_kernel(agg_t, grad_pre, keep_ref, send_ref):
    my_col = lax.axis_index("col")
    core, parity = my_col % 2, (my_col // 2) % 2
    quarter = agg_t.shape[0] // 4
    part = jnp.dot(agg_t[...], grad_pre[...], preferred_element_type=f32).astype(bf16)
    cut = [part[i * quarter : (i + 1) * quarter] for i in range(4)]
    for flip, ref in enumerate((keep_ref, send_ref)):
        here = (core ^ flip) == 0
        first, second = jnp.where(here, cut[0], cut[2]), jnp.where(here, cut[1], cut[3])
        ref[:quarter, :] = jnp.where(parity == 0, first, second)
        ref[quarter:, :] = jnp.where(parity == 0, second, first)


def last_kernel(n_row, grad_agg, *refs):
    backs, quarters, (feat_ref, weight_ref) = refs[:n_row], refs[n_row:-2], refs[-2:]
    feat_ref[...] = (tree_sum([ref[...] for ref in backs]) + grad_agg[...]).astype(bf16)
    my_col = lax.axis_index("col")
    core, parity = my_col % 2, (my_col // 2) % 2
    quarter = quarters[0].shape[0]
    for i, ref in zip((0, 1, 2, 3), quarters):
        at = ((core ^ (i % 2)) * 2 + (parity ^ (i // 2))) * quarter
        weight_ref[pl.ds(pl.multiple_of(at, quarter), quarter), :] = ref[...].astype(f32)


def gather_rows(refs, gathered, order):
    rows, _ = refs[0].shape
    for i, ref in zip(order, refs):
        gathered[i * rows : (i + 1) * rows, :] = ref[...]


def backward_first(n_z, order, *refs):
    st_ref, grads, out, gathered = refs[0], refs[1 : 1 + n_z], refs[-2], refs[-1]
    gather_rows(grads, gathered, order)
    rows = grads[0].shape[0]
    for j in range(out.shape[0] // rows):
        lines = slice(j * rows, (j + 1) * rows)
        out[lines, :] = jnp.dot(st_ref[lines, : n_z * rows], gathered[...], preferred_element_type=f32)


def backward_rest(n_z, n_row, order, *refs):
    st_ref, product, grads, outs, gathered = refs[0], refs[1], refs[2 : 2 + n_z], refs[2 + n_z : -1], refs[-1]
    gather_rows(grads, gathered, order)
    rows = grads[0].shape[0]
    for j, out in enumerate(outs):
        lines = slice(j * rows, (j + 1) * rows)
        other = jnp.dot(st_ref[lines, n_z * rows :], gathered[...], preferred_element_type=f32)
        out[...] = (product[lines, :] + other).astype(out.dtype)


def tree_sum(values):
    values = [x.astype(f32) for x in values]
    while len(values) > 1:
        values = [values[i] + values[i + 1] for i in range(0, len(values), 2)]
    return values[0]


def per_device(features, weight, cotangent, tiles, tile_count, patterns):
    rows, width = features.shape
    slots, words, tile = patterns.shape[2:]
    blocks = rows // tile
    n_row = lax.axis_size("row")
    n_col = lax.axis_size("col")
    n_z = n_col // 2
    row_len = n_z * rows
    col_len = n_row * rows
    flops = 4 * width * col_len * row_len
    high = width + pad_rows

    def over_row(x, k):
        return lax.ppermute(x, "row", [(i, i ^ k) for i in range(n_row)])

    def over_z(x, k):
        return lax.ppermute(x, "col", [(i, i ^ (2 * k)) for i in range(n_col)])

    def over_core(x):
        return lax.ppermute(x, "col", [(i, i ^ 1) for i in range(n_col)])

    feats = [features] + [over_row(features, k) for k in range(1, n_row)]
    (st,) = call(
        functools.partial(build_kernel, blocks, n_z),
        "build",
        [((col_len, 2 * row_len), bf16)],
        [tiles[0, 0], tile_count, patterns[0, 0]],
        n_smem=2,
        anywhere=(2,),
        scratch=[pltpu.VMEM((slots, words, tile), jnp.int32), pltpu.SemaphoreType.DMA],
        flops=4e9,
    )

    n_far = n_z - 2
    sent, feats_t = call(
        functools.partial(forward_first, n_row, n_z + 2),
        "forward_far_other",
        [((n_far, high, rows), bf16), ((high, col_len), bf16)],
        [st] + feats,
        flops=flops // 4,
    )

    def forward(name, start, count):
        return call(
            functools.partial(forward_more, start), name, [((count, high, rows), bf16)], [st, feats_t], flops=flops // 4
        )[0]

    def pair_sum(name, own, other, count):
        return call(pair_kernel, name, [((high, rows), bf16)] * count, [own, other])

    far = pair_sum("pair_far", forward("forward_far_own", 2, n_far), over_core(sent), n_far)
    far = [over_z(x, k) for k, x in enumerate(far, 2)]
    sent = forward("forward_near_other", n_z, 2)
    near = pair_sum("pair_near", forward("forward_near_own", 0, 2), over_core(sent), 2)
    parts = [near[0], over_z(near[1], 1)] + far

    activated, scaled, grad_agg, agg_t, grad_pre = call(
        functools.partial(dense_kernel, n_z),
        "dense",
        [((rows, width), bf16), ((rows, width), bf16), ((rows, width), f32), ((width, rows), bf16), ((rows, width), bf16)],
        parts + [feats_t, cotangent, weight],
        flops=4 * rows * width * width,
    )
    far = [over_z(scaled, k) for k in range(2, n_z)]

    keep, send = call(weight_kernel, "weight_part", [((width // 2, width), bf16)] * 2, [agg_t, grad_pre], flops=2e9)
    half = tree_sum([keep, over_core(send)]).astype(bf16)
    quarter = width // 4
    part = tree_sum([half[:quarter], over_z(half[quarter:], 1)]).astype(bf16)
    part = tree_sum([part] + [over_row(part, k) for k in reversed(range(1, n_row))][::-1]).astype(bf16)
    row_sum = part

    order_own = [0, 1, 2, 3] + list(range(4, n_z))
    order_other = [2, 3, 1, 0] + list(range(4, n_z))
    grads = [scaled, over_z(scaled, 1)] + far
    (product,) = call(
        functools.partial(backward_first, n_z, order_own),
        "backward_own",
        [((col_len, width), f32)],
        [st] + [grads[z] for z in order_own],
        scratch=[pltpu.VMEM((row_len, width), bf16)],
        flops=flops // 2,
    )
    product, part = lax.optimization_barrier((product, row_sum))
    for step in range(1, (n_z - 1).bit_length()):
        part = tree_sum([part, over_z(part, 1 << step)]).astype(bf16)
    backs = call(
        functools.partial(backward_rest, n_z, n_row, order_other),
        "backward_other",
        [((rows, width), bf16)] * n_row,
        [st, product] + [over_core(grads[z]) for z in order_other],
        scratch=[pltpu.VMEM((row_len, width), bf16)],
        flops=flops // 2,
    )
    backs = [backs[0]] + [over_row(backs[k], k) for k in range(1, n_row)]
    straight = lax.ppermute(part, "col", [(i, i ^ 3) for i in range(n_col)])
    grad_features, grad_weight = call(
        functools.partial(last_kernel, n_row),
        "last",
        [((rows, width), bf16), ((width, width), f32)],
        [grad_agg] + backs + [part, over_core(part), over_z(part, 1), straight],
        final=(0, 1),
    )
    return activated, grad_features, grad_weight


def solution(mesh):
    return jax.shard_map(
        per_device,
        mesh=mesh,
        in_specs=(
            P(("row", "col"), None),
            P(),
            P(("row", "col"), None),
            P("row", "col", None, None),
            P("row", "col"),
            P("row", "col", None, None, None),
        ),
        out_specs=(P(("row", "col"), None), P(("row", "col"), None), P()),
        check_vma=False,
    )
```

```python
import functools
import math

import jax
import jax.numpy as jnp
from jax import lax
from jax.experimental import pallas as pl
from jax.experimental.pallas import tpu as pltpu
from jax.sharding import PartitionSpec as P

pad_rows = 16
resident_bytes = 9 << 20
bf16, f32 = jnp.bfloat16, jnp.float32


def fits(shape, dtype):
    return math.prod(shape) * jnp.dtype(dtype).itemsize <= resident_bytes


def smem(count):
    return [pl.BlockSpec(memory_space=pltpu.SMEM)] * count


def call(body, name, outs, args, n_smem=0, anywhere=(), scratch=(), limit=8, flops=1e6, final=()):
    kept = [
        x if i < n_smem or i in anywhere or not fits(x.shape, x.dtype) else pltpu.with_memory_space_constraint(x, pltpu.VMEM)
        for i, x in enumerate(args)
    ]
    shapes = [
        pltpu.VMEM(shape, dtype) if i not in final and fits(shape, dtype) else jax.ShapeDtypeStruct(shape, dtype)
        for i, (shape, dtype) in enumerate(outs)
    ]
    vmem = pl.BlockSpec(memory_space=pltpu.VMEM)
    large = any(not fits(x.shape, x.dtype) for x in args) or any(not fits(*out) for out in outs)
    return pl.pallas_call(
        body,
        out_shape=shapes,
        in_specs=smem(n_smem)
        + [pl.BlockSpec(memory_space=pl.ANY) if i in anywhere else vmem for i in range(n_smem, len(args))],
        out_specs=[vmem] * len(outs),
        scratch_shapes=scratch,
        compiler_params=pltpu.CompilerParams(vmem_limit_bytes=(48 if large else limit) << 20),
        cost_estimate=pl.CostEstimate(flops=int(flops), bytes_accessed=1 << 20, transcendentals=0),
        name=name,
    )(*kept)


def clear(ref):
    rows, width = ref.shape
    step = 128
    zeros = jnp.zeros((step, width), ref.dtype)

    def body(i, _):
        ref[pl.ds(pl.multiple_of(i * step, step), step), :] = zeros
        return 0

    lax.fori_loop(0, rows // step, body, 0)


def unpack_tile(words):
    groups, tile = words.shape
    wide = jnp.broadcast_to(words[:, None, :], (groups, 8, tile))
    shifts = lax.broadcasted_iota(jnp.int32, (groups, 8, tile), 1)
    bits = jnp.bitwise_and(jnp.right_shift(wide, shifts), 1)
    return bits.reshape(groups * 8, tile).astype(jnp.float32).astype(jnp.bfloat16)


def build_kernel(blocks, n_z, tiles, count, patterns, st_ref, held, sem):
    my_row = lax.axis_index("row")
    my_col = lax.axis_index("col")
    my_z, core = my_col // 2, my_col % 2
    tile = patterns.shape[-1]
    copy = pltpu.make_async_copy(patterns, held, sem)
    copy.start()
    clear(st_ref)
    copy.wait()

    def step(t, _):
        a, b = tiles[0, t], tiles[1, t]
        dest = a // blocks
        i0 = ((((dest % 2) ^ core) * n_z + ((dest // 2) ^ my_z)) * blocks + a % blocks) * tile
        k0 = (((b // blocks) ^ my_row) * blocks + b % blocks) * tile
        st_ref[pl.ds(pl.multiple_of(k0, tile), tile), pl.ds(pl.multiple_of(i0, tile), tile)] = unpack_tile(held[t])
        return 0

    lax.fori_loop(0, count[0, 0], step, 0)


def forward_block(feats_t, st_ref, first, rows, width):
    line = lax.broadcasted_iota(jnp.int32, (pad_rows, rows), 0)
    product = jnp.dot(feats_t[...], st_ref[:, first : first + rows], preferred_element_type=f32)
    degree = product[width:]
    high = jnp.floor(degree * (1.0 / 64.0)) * 64.0
    return product[:width].astype(bf16), jnp.where(line == 0, high, jnp.where(line == 1, degree - high, 0.0)).astype(bf16)


def forward_first(n_row, start, *refs):
    st_ref, feats, out, feats_t = refs[0], refs[1 : 1 + n_row], refs[-2], refs[-1]
    rows, width = feats[0].shape
    for i, ref in enumerate(feats):
        feats_t[:width, i * rows : (i + 1) * rows] = ref[...].T
    feats_t[width:, :] = jnp.ones((pad_rows, feats_t.shape[1]), bf16)
    forward_more(start, st_ref, feats_t, out)


def forward_more(start, st_ref, feats_t, out):
    width, rows = out.shape[1] - pad_rows, out.shape[2]
    for j in range(out.shape[0]):
        sums, degree = forward_block(feats_t, st_ref, (start + j) * rows, rows, width)
        out[j, :width, :] = sums
        out[j, width:, :] = degree


def pair_kernel(own, other, *outs):
    for j, out in enumerate(outs):
        out[...] = (own[j].astype(f32) + other[j].astype(f32)).astype(bf16)


def dense_kernel(n_z, *refs):
    parts = refs[:n_z]
    feats, cotangent, weight = refs[n_z : n_z + 3]
    act_ref, scaled_ref, agg_grad_ref, agg_ref, grad_ref = refs[n_z + 3 :]
    width = weight.shape[0]
    total = parts[0][...].astype(f32)
    for part in parts[1:]:
        total = total + part[...].astype(f32)
    degree = total[width : width + 1] + total[width + 1 : width + 2]
    scale = lax.rsqrt(degree + 1.0)
    agg_t = (total[:width] * scale + feats[...].astype(f32).T).astype(bf16)
    agg_ref[...] = agg_t
    w = weight[...]
    preact = jnp.dot(agg_t.T, w, preferred_element_type=f32)
    gate = jax.nn.sigmoid(preact)
    act_ref[...] = (preact * gate).astype(bf16)
    grad_pre = (cotangent[...].astype(f32) * gate * (1.0 + preact * (1.0 - gate))).astype(bf16)
    grad_ref[...] = grad_pre
    grad_agg = lax.dot_general(grad_pre, w, (((1,), (1,)), ((), ())), preferred_element_type=f32)
    agg_grad_ref[...] = grad_agg
    scale_rows = jnp.broadcast_to(scale, agg_t.shape).T
    scaled_ref[...] = (grad_agg * scale_rows).astype(bf16)


def weight_kernel(agg_t, grad_pre, keep_ref, send_ref):
    my_col = lax.axis_index("col")
    core, parity = my_col % 2, (my_col // 2) % 2
    quarter = agg_t.shape[0] // 4
    part = jnp.dot(agg_t[...], grad_pre[...], preferred_element_type=f32).astype(bf16)
    cut = [part[i * quarter : (i + 1) * quarter] for i in range(4)]
    for flip, ref in enumerate((keep_ref, send_ref)):
        here = (core ^ flip) == 0
        first, second = jnp.where(here, cut[0], cut[2]), jnp.where(here, cut[1], cut[3])
        ref[:quarter, :] = jnp.where(parity == 0, first, second)
        ref[quarter:, :] = jnp.where(parity == 0, second, first)


def last_kernel(n_row, grad_agg, *refs):
    backs, quarters, (feat_ref, weight_ref) = refs[:n_row], refs[n_row:-2], refs[-2:]
    feat_ref[...] = (tree_sum([ref[...] for ref in backs]) + grad_agg[...]).astype(bf16)
    my_col = lax.axis_index("col")
    core, parity = my_col % 2, (my_col // 2) % 2
    quarter = quarters[0].shape[0]
    for i, ref in zip((0, 1, 2, 3), quarters):
        at = ((core ^ (i % 2)) * 2 + (parity ^ (i // 2))) * quarter
        weight_ref[pl.ds(pl.multiple_of(at, quarter), quarter), :] = ref[...].astype(f32)


def gather_rows(refs, gathered, order):
    rows, _ = refs[0].shape
    for i, ref in zip(order, refs):
        gathered[i * rows : (i + 1) * rows, :] = ref[...]


def backward_first(n_z, order, *refs):
    st_ref, grads, out, gathered = refs[0], refs[1 : 1 + n_z], refs[-2], refs[-1]
    gather_rows(grads, gathered, order)
    rows = grads[0].shape[0]
    for j in range(out.shape[0] // rows):
        lines = slice(j * rows, (j + 1) * rows)
        out[lines, :] = jnp.dot(st_ref[lines, : n_z * rows], gathered[...], preferred_element_type=f32)


def backward_rest(n_z, n_row, order, *refs):
    st_ref, product, grads, outs, gathered = refs[0], refs[1], refs[2 : 2 + n_z], refs[2 + n_z : -1], refs[-1]
    gather_rows(grads, gathered, order)
    rows = grads[0].shape[0]
    for j, out in enumerate(outs):
        lines = slice(j * rows, (j + 1) * rows)
        other = jnp.dot(st_ref[lines, n_z * rows :], gathered[...], preferred_element_type=f32)
        out[...] = (product[lines, :] + other).astype(out.dtype)


def tree_sum(values):
    values = [x.astype(f32) for x in values]
    while len(values) > 1:
        values = [values[i] + values[i + 1] for i in range(0, len(values), 2)]
    return values[0]


def per_device(features, weight, cotangent, tiles, tile_count, patterns):
    rows, width = features.shape
    slots, words, tile = patterns.shape[2:]
    blocks = rows // tile
    n_row = lax.axis_size("row")
    n_col = lax.axis_size("col")
    n_z = n_col // 2
    row_len = n_z * rows
    col_len = n_row * rows
    flops = 4 * width * col_len * row_len
    high = width + pad_rows

    def over_row(x, k):
        return lax.ppermute(x, "row", [(i, i ^ k) for i in range(n_row)])

    def over_z(x, k):
        return lax.ppermute(x, "col", [(i, i ^ (2 * k)) for i in range(n_col)])

    def over_core(x):
        return lax.ppermute(x, "col", [(i, i ^ 1) for i in range(n_col)])

    feats = [features] + [over_row(features, k) for k in range(1, n_row)]
    (st,) = call(
        functools.partial(build_kernel, blocks, n_z),
        "build",
        [((col_len, 2 * row_len), bf16)],
        [tiles[0, 0], tile_count, patterns[0, 0]],
        n_smem=2,
        anywhere=(2,),
        scratch=[pltpu.VMEM((slots, words, tile), jnp.int32), pltpu.SemaphoreType.DMA],
        flops=4e9,
    )

    n_far = n_z - 2
    sent, feats_t = call(
        functools.partial(forward_first, n_row, n_z + 2),
        "forward_far_other",
        [((n_far, high, rows), bf16), ((high, col_len), bf16)],
        [st] + feats,
        flops=flops // 4,
    )

    def forward(name, start, count):
        return call(
            functools.partial(forward_more, start), name, [((count, high, rows), bf16)], [st, feats_t], flops=flops // 4
        )[0]

    def pair_sum(name, own, other, count):
        return call(pair_kernel, name, [((high, rows), bf16)] * count, [own, other])

    far = pair_sum("pair_far", forward("forward_far_own", 2, n_far), over_core(sent), n_far)
    far = [over_z(x, k) for k, x in enumerate(far, 2)]
    sent = forward("forward_near_other", n_z, 2)
    near = pair_sum("pair_near", forward("forward_near_own", 0, 2), over_core(sent), 2)
    parts = far + [over_z(near[1], 1), near[0]]

    activated, scaled, grad_agg, agg_t, grad_pre = call(
        functools.partial(dense_kernel, n_z),
        "dense",
        [((rows, width), bf16), ((rows, width), bf16), ((rows, width), f32), ((width, rows), bf16), ((rows, width), bf16)],
        parts + [features, cotangent, weight],
        flops=4 * rows * width * width,
    )
    far = [over_z(scaled, k) for k in range(2, n_z)]

    keep, send = call(weight_kernel, "weight_part", [((width // 2, width), bf16)] * 2, [agg_t, grad_pre], flops=2e9)
    half = tree_sum([keep, over_core(send)]).astype(bf16)
    quarter = width // 4
    part = tree_sum([half[:quarter], over_z(half[quarter:], 1)]).astype(bf16)
    part = tree_sum([part] + [over_row(part, k) for k in reversed(range(1, n_row))][::-1]).astype(bf16)
    row_sum = part

    order_own = [0, 1, 2, 3] + list(range(4, n_z))
    order_other = [2, 3, 1, 0] + list(range(4, n_z))
    grads = [scaled, over_z(scaled, 1)] + far
    (product,) = call(
        functools.partial(backward_first, n_z, order_own),
        "backward_own",
        [((col_len, width), f32)],
        [st] + [grads[z] for z in order_own],
        scratch=[pltpu.VMEM((row_len, width), bf16)],
        flops=flops // 2,
    )
    product, part = lax.optimization_barrier((product, row_sum))
    for step in range(1, (n_z - 1).bit_length()):
        part = tree_sum([part, over_z(part, 1 << step)]).astype(bf16)
    backs = call(
        functools.partial(backward_rest, n_z, n_row, order_other),
        "backward_other",
        [((rows, width), bf16)] * n_row,
        [st, product] + [over_core(grads[z]) for z in order_other],
        scratch=[pltpu.VMEM((row_len, width), bf16)],
        flops=flops // 2,
    )
    backs = [backs[0]] + [over_row(backs[k], k) for k in range(1, n_row)]
    straight = lax.ppermute(part, "col", [(i, i ^ 3) for i in range(n_col)])
    grad_features, grad_weight = call(
        functools.partial(last_kernel, n_row),
        "last",
        [((rows, width), bf16), ((width, width), f32)],
        [grad_agg] + backs + [part, over_core(part), over_z(part, 1), straight],
        final=(0, 1),
    )
    return activated, grad_features, grad_weight


def solution(mesh):
    return jax.shard_map(
        per_device,
        mesh=mesh,
        in_specs=(
            P(("row", "col"), None),
            P(),
            P(("row", "col"), None),
            P("row", "col", None, None),
            P("row", "col"),
            P("row", "col", None, None, None),
        ),
        out_specs=(P(("row", "col"), None), P(("row", "col"), None), P()),
        check_vma=False,
    )
```
